256 devices in a mesh: gx: 4 (over x), gy: 2 (over core), gz: 32 (over z, y).
Axes of the slice: x: 4, y: 4, z: 8, core: 2. Of those that a mesh axis runs over, the one named last changes fastest.
Arguments:
- correction: float32 [512, 64, 512], P('gz', 'gx', 'gy'), may hold values from -6 to 6
- residual: float32 [512, 64, 512], P('gz', 'gx', 'gy'), may hold values from -4 to 6
- state: float32 [512, 64, 512], P('gz', 'gx', 'gy'), may hold values from -1 to 1
- spacing_level: int32 [512], replicated, may hold values from 0 to 3
- line_colour: int32 [64, 512], P('gx', 'gy'), may hold values from 0 to 1
Outputs:
- smoothed: float32 [512, 64, 512], P('gz', 'gx', 'gy')
The draws below stay inside these ranges and needn't reach their ends.
All inputs are finite; a program needn't handle non-finite values.
Results may differ from the reference program's by a relative error of at most 0.0003.
Values sent between devices are 32-bit elements; how exact they have to be, the bound alone decides.
No kernel may reach another device: no remote copies, remote signals or barrier semaphores. Data moves between devices by JAX's collectives and lax.ppermute only.
A program may use at most 64 MiB of HBM per device.

```python
import jax
import jax.numpy as jnp
from jax import lax

NZ = 512
NX = 64
NY = 512


def draw_residual(key, part):
    key_noise = jax.random.fold_in(key, 1)
    noise_part = jax.random.normal(key_noise, (NZ, NX, NY), jnp.float32)
    return jnp.clip(1.0 + noise_part, -4.0, 6.0)


def with_ends(drawn, rng, least, largest):
    longest = drawn.shape.index(max(drawn.shape))
    spots = []
    for shift in (0, 1):
        where = [jax.random.randint(jax.random.fold_in(rng, axis), (), 0, length) for axis, length in enumerate(drawn.shape)]
        where[longest] = (where[longest] + shift) % drawn.shape[longest]
        spots.append(tuple(where))
    return drawn.at[spots[0]].set(least).at[spots[1]].set(largest)


def steps_of(stream_key, extent, shards, low, top_value):
    loudness = 1.0
    for dim, blocks in shards:
        steps = jax.random.uniform(jax.random.fold_in(jax.random.fold_in(stream_key, 6), dim), (blocks,), jnp.float32, low / len(shards), top_value / len(shards))
        loudness = loudness * jnp.repeat(jnp.exp(steps), extent[dim] // blocks).reshape((-1,) + (1,) * (len(extent) - 1 - dim))
    return loudness


def noise(rng, shape, spread, most, cuts=(), kind=jnp.bfloat16):
    result = jax.random.normal(rng, shape, jnp.float32) * spread
    if len(cuts) > 0:
        result = steps_of(rng, shape, cuts, -0.22, 0.18) * result
    return jnp.clip(result, min=-most, max=most).astype(kind)


def setup_inputs(seed: int = 0) -> dict:
    arg_keys = jax.random.split(jax.random.key(seed), 6)
    return {
        "correction": noise(arg_keys[0], (NZ, NX, NY), 1.0, 6.0, ((0, 32), (1, 4), (2, 2)), jnp.float32),
        "residual": draw_residual(jax.random.fold_in(arg_keys[5], 71), 0),
        "state": jnp.clip(jax.random.uniform(arg_keys[2], (NZ, NX, NY), jnp.float32, -1.0, 1.0) * steps_of(arg_keys[2], (NZ, NX, NY), ((0, 32), (1, 4), (2, 2)), -0.4, 0.0), -1.0, 1.0),
        "spacing_level": with_ends(jax.random.randint(arg_keys[3], (NZ,), 0, 4), jax.random.fold_in(arg_keys[3], 1), 0, 3).astype(jnp.int32),
        "line_colour": with_ends(jax.random.randint(arg_keys[4], (NX, NY), 0, 2), jax.random.fold_in(arg_keys[4], 1), 0, 1).astype(jnp.int32),
    }


coef_z = 1000.0
coef_x = 0.3
coef_y = 0.2
bratu_lambda = 0.2


def face_coupling(spacing_level):
    spacing_cells = 0.8 * jnp.power(1.3, spacing_level.astype(jnp.float32))
    inner_faces = coef_z * 2.0 / (spacing_cells[:-1] + spacing_cells[1:])
    nothing = jnp.zeros((1,), jnp.float32)
    face_low = jnp.concatenate([nothing, inner_faces])
    face_high = jnp.concatenate([inner_faces, nothing])
    return spacing_cells, face_low, face_high


def thomas_solve(below_coef, centre, above_coef, source):
    def forward(state_carry, row_data):
        prev_ratio, prev_value = state_carry
        low_term, mid_term, high_term, src_term = row_data
        pivot_value = mid_term - low_term * prev_ratio
        ratio_now = high_term / pivot_value
        value_now = (src_term - low_term * prev_value) / pivot_value
        return (ratio_now, value_now), (ratio_now, value_now)

    blank = jnp.zeros(centre.shape[1:], jnp.float32)
    unused_end, (ratios, values) = lax.scan(forward, (blank, blank), (below_coef, centre, above_coef, source))

    def backward(next_value, row_data):
        ratio_now, value_now = row_data
        result_now = value_now - ratio_now * next_value
        return result_now, result_now

    unused_start, solution = lax.scan(backward, blank, (ratios, values), reverse=True)
    return solution


def reference(correction, residual, state, spacing_level, line_colour):
    spacing_cells, face_low, face_high = face_coupling(spacing_level)
    column = spacing_cells[:, None, None]
    centre = (face_low + face_high)[:, None, None] + column * (2.0 * coef_x + 2.0 * coef_y - bratu_lambda * jnp.exp(state))
    iterate = correction
    for colour in range(2):
        padded = jnp.pad(iterate, ((0, 0), (1, 1), (1, 1)))
        beside = coef_x * (padded[:, 2:, 1:-1] + padded[:, :-2, 1:-1]) + coef_y * (padded[:, 1:-1, 2:] + padded[:, 1:-1, :-2])
        source = column * (residual + beside)
        solved = thomas_solve(-face_low, centre, -face_high, source)
        iterate = jnp.where((line_colour == colour)[None], solved, iterate)
    return iterate
```

```python
import jax
import jax.numpy as jnp
from jax import lax
from jax.experimental import pallas as pl
from jax.experimental.pallas import tpu as pltpu
from jax.sharding import PartitionSpec as P

coef_z = 1000.0
coef_x = 0.3
coef_y = 0.2
bratu_lambda = 0.2

D = 16
X = 16
Y = 256
L = 128
B = 32
R = 32

XHI, YH, XLO0, OWN15, YOWN, XLO1 = 0, 2, 3, 4, 6, 7
WXM, WXP, WYP = 20, 24, 28


def iota(shape, dim):
    return lax.broadcasted_iota(jnp.int32, shape, dim)


def row_coefficients(level_ref):
    base = lax.axis_index("gz") * D
    last = level_ref.shape[0] - 1

    def spacing(row):
        level = level_ref[jnp.clip(base + row, 0, last)]
        once = jnp.where((level & 1) == 1, jnp.float32(1.3), jnp.float32(1.0))
        twice = jnp.where((level & 2) == 2, jnp.float32(1.3 * 1.3), jnp.float32(1.0))
        return jnp.float32(0.8) * (once * twice)

    around = [spacing(row) for row in range(-1, D + 1)]
    faces = []
    for i in range(D + 1):
        inside = (base + i > 0) & (base + i <= last)
        face = jnp.float32(coef_z * 2.0) / (around[i] + around[i + 1])
        faces.append(jnp.where(inside, face, jnp.float32(0.0)))
    return around[1 : D + 1], faces


def centre_of(spacing, low, high, state):
    return (low + high) + spacing * ((2.0 * coef_x + 2.0 * coef_y) - bratu_lambda * jnp.exp(state))


def transposed(rows):
    short = L - rows.shape[0]
    if short:
        rows = jnp.concatenate([rows, jnp.zeros((short, L), rows.dtype)], 0)
    return jnp.transpose(rows)


def at(k):
    return slice(k * X, (k + 1) * X)


def beside_after_first(face, h_source, h_inv, low, high, h_line):
    value = low
    forwards = []
    for k in range(D - 1):
        rows = slice(k * 8, (k + 1) * 8)
        value = (h_source[rows, :] + face[k] * value) * h_inv[rows, :]
        forwards.append(value)
    value = high
    h_line[(D - 1) * 8 :, :] = value
    for k in range(D - 2, -1, -1):
        rows = slice(k * 8, (k + 1) * 8)
        value = forwards[k] + (face[k + 1] * h_inv[rows, :]) * value
        h_line[rows, :] = value


def own_after_first(face, source, inv, tint, low, high, v_first):
    value = low
    for k in range(D - 1):
        value = (source[at(k), :] + face[k] * value) * inv[at(k), :]
        v_first[at(k), :] = value
    value = high
    for k in range(D - 1, -1, -1):
        if k < D - 1:
            value = v_first[at(k), :] + (face[k + 1] * inv[at(k), :]) * value
        v_first[at(k), :] = jnp.where(tint == 0, value, 0.0)


def beside_sum(v_first, h_line, column, k, left_core):
    row, lane = iota((X, Y), 0), iota((X, Y), 1)
    lines = v_first[at(k), :]
    sides = h_line[k * 8 : (k + 1) * 8, :]
    lo = jnp.concatenate([sides[XLO0 : XLO0 + 1], sides[XLO1 : XLO1 + 1]], 1)
    hi = jnp.concatenate([sides[XHI : XHI + 1], sides[XHI + 1 : XHI + 2]], 1)

    left = jnp.where(lane == 0, jnp.where(left_core, 0.0, column), pltpu.roll(lines, 1, 1))
    right = jnp.where(
        lane == Y - 1, jnp.where(left_core, column, 0.0), pltpu.roll(lines, Y - 1, 1)
    )
    in_x = jnp.where(row == 0, lo, pltpu.roll(lines, 1, 0)) + jnp.where(
        row == X - 1, hi, pltpu.roll(lines, X - 1, 0)
    )
    return coef_x * in_x + coef_y * (left + right)


def pack_x_kernel(corr, res, state, colour, lo, hi):
    for out, edge, inner in ((lo, 0, 1), (hi, X - 1, X - 2)):
        for i, (ref, x) in enumerate(((corr, edge), (corr, inner), (res, edge), (state, edge))):
            for k in range(D):
                out[i * D + k : i * D + k + 1, :] = ref[k * X + x : k * X + x + 1, :]
        row = colour[edge : edge + 1, :].astype(jnp.float32)
        out[4 * D : 4 * D + 8, :] = jnp.broadcast_to(row, (8, Y))


def pack_y_kernel(corr, res, state, colour, after, out):
    left_core = lax.axis_index("gy") == 0

    def columns(value):
        near = jnp.where(left_core, value[:, L:], value[:, :L])
        return jnp.concatenate([transposed(near[i : i + L]) for i in range(0, near.shape[0], L)], 1)

    def picked(turned, inner):
        return jnp.where(left_core, turned[L - 1 - inner : L - inner], turned[inner : inner + 1])

    field = columns(corr[...])
    out[0:1, :] = picked(field, 0)
    out[1:2, :] = picked(field, 1)
    out[2:3, :] = picked(columns(res[...]), 0)
    out[3:4, :] = picked(columns(state[...]), 0)
    row = picked(columns(colour[...].astype(jnp.float32)), 0)
    out[4:8, :] = jnp.broadcast_to(jnp.concatenate([row, row], 1), (4, Y))


def factor_kernel(level, state, inv, e_first, e_last, k_own, w_x, w_y):
    spacing, face = row_coefficients(level)

    def rows(ref, k):
        return ref[k * X : (k + 1) * X, :]

    ratios, forward = [], []
    ratio = running = None
    for k in range(D - 1):
        pivot = centre_of(spacing[k], face[k], face[k + 1], rows(state, k))
        if k:
            pivot = pivot - face[k] * ratio
        inverse = 1.0 / pivot
        scaled = face[k] * inverse
        running = scaled * running if k else scaled
        ratio = face[k + 1] * inverse
        inv[k * X : (k + 1) * X, :] = inverse
        e_first[k * X : (k + 1) * X, :] = running
    inv[(D - 1) * X :, :] = jnp.zeros((X, Y), jnp.float32)
    e_first[(D - 1) * X :, :] = jnp.zeros((X, Y), jnp.float32)
    e_last[(D - 1) * X :, :] = jnp.ones((X, Y), jnp.float32)
    zero, one = jnp.zeros((X, Y), jnp.float32), jnp.ones((X, Y), jnp.float32)
    first, last = zero, one
    wx = [zero, zero, zero, one * (coef_x * spacing[D - 1])]
    wy = [zero, zero, zero, one * (coef_y * spacing[D - 1])]
    for k in range(D - 2, -1, -1):
        ratio = face[k + 1] * rows(inv, k)
        first = rows(e_first, k) + ratio * first
        last = ratio * last
        e_first[k * X : (k + 1) * X, :] = first
        e_last[k * X : (k + 1) * X, :] = last
        if k == D - 2:
            k_own[X : 2 * X, :] = face[D - 1] * first
            centre = centre_of(spacing[D - 1], face[D - 1], face[D], rows(state, D - 1))
            k_own[2 * X :, :] = centre - face[D - 1] * last
        before = (pltpu.roll(first, 1, 0), pltpu.roll(last, 1, 0))
        after = (pltpu.roll(first, Y - 1, 1), pltpu.roll(last, Y - 1, 1))
        for a, mine in enumerate((first, last)):
            in_x, in_y = (coef_x * spacing[k]) * mine, (coef_y * spacing[k]) * mine
            for b in range(2):
                wx[2 * a + b] = wx[2 * a + b] + in_x * before[b]
                wy[2 * a + b] = wy[2 * a + b] + in_y * after[b]
    k_own[:X, :] = face[0] * first
    for i in range(4):
        w_x[i * X : (i + 1) * X, :] = wx[i]
        w_y[i * X : (i + 1) * X, :] = wy[i]


def interface_kernel(
    level, corr, res, colour, inv, e_first, e_last, k_own, w_x, w_y,
    own_lo, own_hi, got_lo, got_hi, own_y, got_y, cross_lo, cross_hi,
    message, source, h_source, h_inv,
    y_scratch, h_state, h_before, h_first, h_last, h_line, v_first,
):
    spacing, face = row_coefficients(level)
    left_core = lax.axis_index("gy") == 0
    has_lo, has_hi = lax.axis_index("gx") > 0, lax.axis_index("gx") < lax.axis_size("gx") - 1
    row = iota((X, Y), 0)
    lane = iota((X, Y), 1)

    def plane(ref, i):
        return ref[i * D : (i + 1) * D, :]

    def spread(ref):
        for k in range(D):
            at = k % 8 * X
            tile = ref[:, k // 8 * L : (k // 8 + 1) * L]
            y_scratch[k * 8 : (k + 1) * 8, :] = pltpu.roll(tile, L - at, 1) if at else tile
        return [y_scratch[pl.ds(q, D, stride=8), :] for q in range(5)]

    yh_corr, yh_next, yh_res, yh_state, yh_colour = spread(got_y)
    yo_corr, unused, unused, yo_state, unused = spread(own_y)
    yh_colour = yh_colour[0:1]

    small_lane = iota((D, L), 1)

    def corner(ref, there):
        value = jnp.where(left_core, ref[:, 0:1], ref[:, Y - 1 : Y])
        return jnp.where(there, value, 0.0)

    corner_lo, corner_hi = corner(cross_lo, has_lo), corner(cross_hi, has_hi)

    h_state[...] = jnp.zeros_like(h_state)
    h_before[...] = jnp.zeros_like(h_before)

    below = jnp.where(small_lane == 0, corner_lo, pltpu.roll(yh_corr, 1, 1))
    above = jnp.where(small_lane == X - 1, corner_hi, pltpu.roll(yh_corr, L - 1, 1))
    yh_source = yh_res + (coef_x * (below + above) + coef_y * (yo_corr + yh_next))
    h_before[pl.ds(YH, D, stride=8), :] = jnp.where(yh_colour == 0.0, yh_source, 0.0)
    h_state[pl.ds(YH, D, stride=8), :] = yh_state
    h_state[pl.ds(YOWN, D, stride=8), :] = yo_state
    beside_corr = []
    row_k = iota((D, Y), 0)
    lane_k = iota((D, Y), 1)
    for got, own, there, at_corner, places in (
        (got_lo, own_lo, has_lo, corner_lo, (XLO0, XLO1)),
        (got_hi, own_hi, has_hi, corner_hi, (XHI, XHI + 1)),
    ):
        near = jnp.where(there, plane(got, 0), 0.0)
        beside_corr.append(near)
        left = jnp.where(lane_k == 0, jnp.where(left_core, 0.0, at_corner), pltpu.roll(near, 1, 1))
        right = jnp.where(
            lane_k == Y - 1, jnp.where(left_core, at_corner, 0.0), pltpu.roll(near, Y - 1, 1)
        )
        value = plane(got, 2) + (coef_x * (plane(got, 1) + plane(own, 0)) + coef_y * (left + right))
        value = jnp.where(there & (got[4 * D : 4 * D + 1, :] == 0.0), value, 0.0)
        states = plane(got, 3)
        for c, place in enumerate(places):
            h_before[pl.ds(place, D, stride=8), :] = value[:, c * L : (c + 1) * L]
            h_state[pl.ds(place, D, stride=8), :] = states[:, c * L : (c + 1) * L]
    edge_state = plane(own_hi, 3)
    for c in range(2):
        h_state[pl.ds(OWN15 + c, D, stride=8), :] = edge_state[:, c * L : (c + 1) * L]

    def rows8(ref, k):
        return ref[k * 8 : (k + 1) * 8, :]

    ratio = running = None
    inverses, forwards = [], []
    for k in range(D - 1):
        pivot = centre_of(spacing[k], face[k], face[k + 1], rows8(h_state, k))
        if k:
            pivot = pivot - face[k] * ratio
        inverse = 1.0 / pivot
        scaled = face[k] * inverse
        running = scaled * running if k else scaled
        ratio = face[k + 1] * inverse
        inverses.append(inverse)
        forwards.append(running)
        h_inv[k * 8 : (k + 1) * 8, :] = inverse
    h_inv[(D - 1) * 8 :, :] = jnp.zeros((8, L), jnp.float32)
    zero, one = jnp.zeros((8, L), jnp.float32), jnp.ones((8, L), jnp.float32)
    place8 = iota((8, L), 0)
    weight = jnp.where((place8 == YOWN) | (place8 == YH), jnp.float32(coef_y), jnp.float32(coef_x))
    first, last = zero, one
    hw = [zero, zero, zero, weight * spacing[D - 1]]
    hs = spacing[D - 1] * rows8(h_before, D - 1)
    h_source[(D - 1) * 8 :, :] = hs
    hf = [zero, hs]
    hk = [None, None, None]
    h_first[(D - 1) * 8 :, :] = zero
    h_last[(D - 1) * 8 :, :] = one * (coef_x * spacing[D - 1])
    for k in range(D - 2, -1, -1):
        ratio = face[k + 1] * inverses[k]
        first = forwards[k] + ratio * first
        last = ratio * last
        if k == D - 2:
            hk[1] = face[D - 1] * first
            centre = centre_of(spacing[D - 1], face[D - 1], face[D], rows8(h_state, D - 1))
            hk[2] = centre - face[D - 1] * last
        hs = spacing[k] * rows8(h_before, k)
        h_source[k * 8 : (k + 1) * 8, :] = hs
        hf[0] = hf[0] + first * hs
        hf[1] = hf[1] + last * hs
        h_first[k * 8 : (k + 1) * 8, :] = (coef_x * spacing[k]) * first
        h_last[k * 8 : (k + 1) * 8, :] = (coef_x * spacing[k]) * last
        partner = (pltpu.roll(first, 4, 0), pltpu.roll(last, 4, 0))
        for a, mine in enumerate((first, last)):
            mine = (weight * spacing[k]) * mine
            for b in range(2):
                hw[2 * a + b] = hw[2 * a + b] + mine * partner[b]
    hk[0] = face[0] * first

    columns = transposed(
        jnp.concatenate(
            [v[YH : YH + 1] for v in hk + hf] + [v[YOWN : YOWN + 1] for v in hw], 0
        )
    )
    columns_corr = transposed(jnp.concatenate([yh_corr, yh_colour], 0))

    mine = colour[...]
    colour_lo, colour_hi = got_lo[4 * D : 4 * D + 1, :], got_hi[4 * D : 4 * D + 1, :]
    tint = mine.astype(jnp.float32)
    tint_y = columns_corr[:X, D : D + 1]
    at_left, at_right = (lane == 0), (lane == Y - 1)

    def beside_of(value, lo, hi, y_column):
        return (
            jnp.where(row == 0, lo, pltpu.roll(value, 1, 0)),
            jnp.where(row == X - 1, hi, pltpu.roll(value, X - 1, 0)),
            jnp.where(at_left, jnp.where(left_core, 0.0, y_column), pltpu.roll(value, 1, 1)),
            jnp.where(at_right, jnp.where(left_core, y_column, 0.0), pltpu.roll(value, Y - 1, 1)),
        )

    weights = [
        jnp.where((tint == 1.0) & (other == 0.0), 0.0, jnp.float32(amount))
        for other, amount in zip(
            beside_of(tint, colour_lo, colour_hi, tint_y), (coef_x, coef_x, coef_y, coef_y)
        )
    ]
    for k in range(D):
        value = corr[k * X : (k + 1) * X, :]
        around = beside_of(
            value, beside_corr[0][k : k + 1], beside_corr[1][k : k + 1], columns_corr[:X, k : k + 1]
        )
        total = res[k * X : (k + 1) * X, :]
        for w, v in zip(weights, around):
            total = total + w * v
        source[at(k), :] = spacing[k] * total

    beside_after_first(face, h_source, h_inv, zero, zero, h_line)
    still = jnp.zeros((X, Y), jnp.float32)
    own_after_first(face, source, inv, mine, still, still, v_first)
    columns_first = transposed(h_line[pl.ds(YH, D, stride=8), :])
    f_first = f_last = still
    for k in range(D):
        added = beside_sum(v_first, h_line, columns_first[:X, k : k + 1], k, left_core)
        total = source[at(k), :] + jnp.where(mine == 1, spacing[k] * added, 0.0)
        f_first = f_first + e_first[at(k), :] * total
        f_last = f_last + e_last[at(k), :] * total

    def put(r, half, value):
        message[pl.ds(half * R + r, X, stride=2 * R), :] = value

    def put_both(r, value):
        put(r, 0, value[:, :L])
        put(r, 1, value[:, L:])

    short_lane = iota((X, L), 1)
    own_values = [k_own[i * X : (i + 1) * X, :] for i in range(3)] + [f_first, f_last]
    seen_values = own_values[:3] + [jnp.where(tint == 0.0, f, still) for f in own_values[3:]]
    inner_link = [w_y[i * X : (i + 1) * X, :][:, L - 1 : L] for i in (0, 2, 1, 3)]
    for q in range(5):
        own, seen = own_values[q], seen_values[q]
        side = (hk + hf)[q]
        put_both(4 * q, own)
        low = jnp.concatenate([side[XLO0 : XLO0 + 1], side[XLO1 : XLO1 + 1]], 1)
        high = jnp.concatenate([side[XHI : XHI + 1], side[XHI + 1 : XHI + 2]], 1)
        put_both(4 * q + 1, jnp.where(row == 0, low, pltpu.roll(seen, 1, 0)))
        put_both(4 * q + 2, jnp.where(row == X - 1, high, pltpu.roll(seen, X - 1, 0)))
        outer = columns[:X, q : q + 1]
        left_end, right_end = seen[:, L:], seen[:, :L]
        left_none, right_none = (0.0, 0.0) if q >= 3 else (left_end, right_end)
        left_end = jnp.where(
            short_lane == L - 1, jnp.where(left_core, left_none, outer), left_end
        )
        right_end = jnp.where(short_lane == 0, jnp.where(left_core, outer, right_none), right_end)
        if q < 4:
            link = columns[:X, 5 + q : 6 + q]
            left_end = jnp.where(short_lane == L // 2, jnp.where(left_core, 0.0, link), left_end)
            right_end = jnp.where(short_lane == L // 2, inner_link[q], right_end)
        put(4 * q + 3, 0, left_end)
        put(4 * q + 3, 1, right_end)

    edge_first, edge_last = (
        jnp.concatenate([e[k * X : k * X + 1, :] for k in range(D)], 0) for e in (e_first, e_last)
    )
    low_first = jnp.concatenate([h_first[pl.ds(p, D, stride=8), :] for p in (XLO0, XLO1)], 1)
    low_last = jnp.concatenate([h_last[pl.ds(p, D, stride=8), :] for p in (XLO0, XLO1)], 1)
    for a, mine_e in enumerate((edge_first, edge_last)):
        for b, other_e in enumerate((low_first, low_last)):
            i, j = 2 * a + b, 2 * b + a
            edge = jnp.sum(mine_e * other_e, axis=0, keepdims=True)
            put_both(WXM + i, jnp.where(row == 0, edge, w_x[i * X : (i + 1) * X, :]))
            high = jnp.concatenate([hw[i][OWN15 : OWN15 + 1], hw[i][OWN15 + 1 : OWN15 + 2]], 1)
            turned = pltpu.roll(w_x[j * X : (j + 1) * X, :], X - 1, 0)
            put_both(WXP + i, jnp.where(row == X - 1, high, turned))
            link = jnp.where(left_core, columns[:X, 5 + i : 6 + i], 0.0)
            put_both(WYP + i, jnp.where(at_right, link, w_y[i * X : (i + 1) * X, :]))


def separator_kernel(got, colour, out, v_scratch, line_scratch):
    patch = lax.axis_index("gz")
    tint = colour[pl.ds(patch // 2, 1), :]
    tint = jnp.where(patch % 2 == 0, tint[:, :L], tint[:, L:])

    def quantity(q, d):
        return got[d * R + 4 * q : d * R + 4 * q + 4, :]

    off = [quantity(1, d) for d in range(B)]
    diag = [
        quantity(2, d) - quantity(0, d + 1) if d < B - 1 else quantity(2, d) for d in range(B)
    ]
    right = [
        quantity(4, d) + quantity(3, d + 1) if d < B - 1 else quantity(4, d) for d in range(B)
    ]
    middle = B // 2
    up, down = {}, {}
    for n in range(middle):
        d = n
        pivot = diag[d] - off[d] * up[d - 1][1] if n else diag[d]
        inverse = 1.0 / pivot
        up[d] = (inverse, off[d + 1] * inverse)
        d = B - 1 - n
        if d > middle:
            pivot = diag[d] - off[d + 1] * down[d + 1][1] if n else diag[d]
            inverse = 1.0 / pivot
            down[d] = (inverse, off[d] * inverse)
    centre = diag[middle] - off[middle] * up[middle - 1][1] - off[middle + 1] * down[middle + 1][1]
    centre = 1.0 / centre

    def solved(right, sets):
        def cut(value):
            return value[:sets]

        ahead, behind, values = {}, {}, [None] * B
        for n in range(middle):
            d = n
            total = right[d] + cut(off[d]) * ahead[d - 1] if n else right[d]
            ahead[d] = total * cut(up[d][0])
            d = B - 1 - n
            if d > middle:
                total = right[d] + cut(off[d + 1]) * behind[d + 1] if n else right[d]
                behind[d] = total * cut(down[d][0])
        total = (
            right[middle]
            + cut(off[middle]) * ahead[middle - 1]
            + cut(off[middle + 1]) * behind[middle + 1]
        )
        values[middle] = total * cut(centre)
        for n in range(middle):
            d = middle - 1 - n
            values[d] = ahead[d] + cut(up[d][1]) * values[d + 1]
            d = middle + 1 + n
            if d < B:
                values[d] = behind[d] + cut(down[d][1]) * values[d - 1]
        return values

    v_scratch[0:4, :] = jnp.zeros((4, L), jnp.float32)
    for d, value in enumerate(solved(right, 4)):
        v_scratch[4 + d * 4 : 8 + d * 4, :] = value

    lane = iota((B, L), 1)

    def of_set(s):
        return v_scratch[pl.ds(s, B, stride=4), :], v_scratch[pl.ds(4 + s, B, stride=4), :]

    def lines(r):
        return got[pl.ds(r, B, stride=R), :]

    own_pair, lo_pair, hi_pair, end_pair = (of_set(s) for s in range(4))
    first_pair = [jnp.where(tint == 0, v, 0.0) for v in own_pair]
    left_pair = [
        jnp.where(lane == 0, pltpu.roll(e, 1, 1), pltpu.roll(v, 1, 1))
        for e, v in zip(end_pair, first_pair)
    ]
    right_pair = [
        jnp.where(lane == L - 1, pltpu.roll(e, L - 1, 1), pltpu.roll(v, L - 1, 1))
        for e, v in zip(end_pair, first_pair)
    ]
    added = []
    for a in range(2):
        total = jnp.zeros((B, L), jnp.float32)
        for b in range(2):
            i, j = 2 * a + b, 2 * b + a
            total = total + lines(WXM + i) * lo_pair[b]
            total = total + lines(WXP + i) * hi_pair[b]
            total = total + lines(WYP + i) * right_pair[b]
            back = jnp.where(
                lane == 0, pltpu.roll(lines(4 * i + 3), L // 2, 1), pltpu.roll(lines(WYP + j), 1, 1)
            )
            total = total + back * left_pair[b]
        added.append(jnp.where(tint == 1, total, 0.0) + lines(12 + 4 * a))
    line_scratch[0:B, :] = added[0]
    line_scratch[B : B + 8, :] = jnp.zeros((8, L), jnp.float32)
    line_scratch[0:B, :] = added[1] + line_scratch[1 : B + 1, :]
    second = [line_scratch[d : d + 1, :] for d in range(B)]
    values = solved(second, 1)
    line_scratch[0:1, :] = jnp.zeros((1, L), jnp.float32)
    for d in range(B):
        line_scratch[d + 1 : d + 2, :] = values[d]
    results = [line_scratch[0:B, :], line_scratch[1 : B + 1, :]]
    results += [*lo_pair, *hi_pair, *end_pair]
    for i, value in enumerate(results):
        out[pl.ds(i, B, stride=8), :] = value


def finish_kernel(level, source, inv, h_source, h_inv, colour, got, out, v_first, h_line):
    spacing, face = row_coefficients(level)
    left_core = lax.axis_index("gy") == 0
    mine = colour[...]

    def own(i):
        return jnp.concatenate([got[pl.ds(h * 8 + i, X, stride=16), :] for h in range(2)], 1)

    low, high = own(0), own(1)
    ends = []
    for i in (6, 7):
        near = got[pl.ds(8 + i, X, stride=16), :]
        far = pltpu.roll(got[pl.ds(i, X, stride=16), :], 1, 1)
        ends.append(jnp.where(left_core, near, far)[:, 0:1])
    short_lane = iota((X, L), 1)
    pair = jnp.where(short_lane == 0, ends[0], ends[1])
    turned = transposed(pair)
    nothing = jnp.zeros((1, L), jnp.float32)

    def beside(b):
        at = {XHI: 30 * 8 + 4, XHI + 1: 31 * 8 + 4, XLO0: 2, XLO1: 8 + 2}
        rows = [
            turned[b : b + 1]
            if p == YH
            else got[at[p] + b : at[p] + b + 1, :]
            if p in at
            else nothing
            for p in range(8)
        ]
        return jnp.concatenate(rows, 0)

    beside_after_first(face, h_source, h_inv, beside(0), beside(1), h_line)
    columns = transposed(h_line[pl.ds(YH, D, stride=8), :])
    own_after_first(face, source, inv, mine, low, high, v_first)
    value = low
    for k in range(D - 1):
        added = beside_sum(v_first, h_line, columns[:X, k : k + 1], k, left_core)
        value = (source[at(k), :] + spacing[k] * added + face[k] * value) * inv[at(k), :]
        out[at(k), :] = value
    value = high
    for k in range(D - 1, -1, -1):
        if k < D - 1:
            value = out[at(k), :] + (face[k + 1] * inv[at(k), :]) * value
        out[at(k), :] = jnp.where(mine == 0, v_first[at(k), :], value)


VMEM = pl.BlockSpec(memory_space=pltpu.VMEM)
SMEM = pl.BlockSpec(memory_space=pltpu.SMEM)


def f32(*shape):
    return jax.ShapeDtypeStruct(shape, jnp.float32)


def call(kernel, outs, specs, scratch, cost, *args):
    return pl.pallas_call(
        kernel,
        out_shape=outs,
        in_specs=specs,
        out_specs=jax.tree.map(lambda _: VMEM, outs),
        scratch_shapes=[pltpu.VMEM(shape, jnp.float32) for shape in scratch],
        compiler_params=pltpu.CompilerParams(vmem_limit_bytes=32 * 1024 * 1024),
        cost_estimate=pl.CostEstimate(flops=cost, bytes_accessed=cost, transcendentals=0),
    )(*args)


def on_device(correction, residual, state, level, colour):
    corr, res, st = (v.reshape(D * X, Y) for v in (correction, residual, state))
    own_lo, own_hi = call(
        pack_x_kernel, (f32(72, Y), f32(72, Y)), [VMEM] * 4, [], 1 << 20, corr, res, st, colour
    )
    xs = lax.axis_size("gx")
    ring = [(i, (i + 1) % xs) for i in range(xs)]
    got_lo = lax.ppermute(own_hi, "gx", ring)
    got_hi = lax.ppermute(own_lo, "gx", [(b, a) for a, b in ring])
    own_y = call(
        pack_y_kernel, f32(8, Y), [VMEM] * 4 + [pl.BlockSpec(memory_space=pl.ANY)], [],
        1 << 20, corr, res, st, colour, own_lo,
    )
    swap = [(0, 1), (1, 0)]
    got_y = lax.ppermute(own_y, "gy", swap)
    field = f32(D * X, Y)
    inv, e_first, e_last, k_own, w_x, w_y = call(
        factor_kernel, (field, field, field, f32(3 * X, Y), f32(4 * X, Y), f32(4 * X, Y)),
        [SMEM, VMEM], [], 1 << 22, level, st,
    )
    cross_lo = lax.ppermute(got_lo[:D], "gy", swap)
    cross_hi = lax.ppermute(got_hi[:D], "gy", swap)
    message, source, h_source, h_inv = call(
        interface_kernel, (f32(B * R, L), field, f32(8 * D, L), f32(8 * D, L)),
        [SMEM] + [VMEM] * 17, [(8 * D, L)] * 6 + [(D * X, Y)], 1 << 22,
        level, corr, res, colour, inv, e_first, e_last, k_own, w_x, w_y,
        own_lo, own_hi, got_lo, got_hi, own_y, got_y, cross_lo, cross_hi,
    )

    def exchanged(value, rows):
        blocks = value.reshape(B, rows, L)
        return lax.all_to_all(blocks, "gz", 0, 0, tiled=True).reshape(B * rows, L)

    separators = call(
        separator_kernel, f32(B * 8, L), [VMEM] * 2, [(4 * B + 8, L), (B + 8, L)],
        1 << 21, exchanged(message, R), colour,
    )
    out = call(
        finish_kernel, field, [SMEM] + [VMEM] * 6, [(D * X, Y), (8 * D, L)], 1 << 21,
        level, source, inv, h_source, h_inv, colour, exchanged(separators, 8),
    )
    return out.reshape(D, X, Y)


def solution(mesh):
    block = P("gz", "gx", "gy")
    return jax.shard_map(
        on_device,
        mesh=mesh,
        in_specs=(block, block, block, P(), P("gx", "gy")),
        out_specs=block,
        check_vma=False,
    )
```

```python
import jax
import jax.numpy as jnp
from jax import lax
from jax.experimental import pallas as pl
from jax.experimental.pallas import tpu as pltpu
from jax.sharding import PartitionSpec as P

coef_z = 1000.0
coef_x = 0.3
coef_y = 0.2
bratu_lambda = 0.2

D = 16
X = 16
Y = 256
L = 128
B = 32
R = 32

XHI, YH, XLO0, OWN15, YOWN, XLO1 = 0, 2, 3, 4, 6, 7
WXM, WXP, WYP = 20, 24, 28


def iota(shape, dim):
    return lax.broadcasted_iota(jnp.int32, shape, dim)


def row_coefficients(level_ref):
    base = lax.axis_index("gz") * D
    last = level_ref.shape[0] - 1

    def spacing(row):
        level = level_ref[jnp.clip(base + row, 0, last)]
        once = jnp.where((level & 1) == 1, jnp.float32(1.3), jnp.float32(1.0))
        twice = jnp.where((level & 2) == 2, jnp.float32(1.3 * 1.3), jnp.float32(1.0))
        return jnp.float32(0.8) * (once * twice)

    around = [spacing(row) for row in range(-1, D + 1)]
    faces = []
    for i in range(D + 1):
        inside = (base + i > 0) & (base + i <= last)
        face = jnp.float32(coef_z * 2.0) / (around[i] + around[i + 1])
        faces.append(jnp.where(inside, face, jnp.float32(0.0)))
    return around[1 : D + 1], faces


def centre_of(spacing, low, high, state):
    return (low + high) + spacing * ((2.0 * coef_x + 2.0 * coef_y) - bratu_lambda * jnp.exp(state))


def transposed(rows):
    short = L - rows.shape[0]
    if short:
        rows = jnp.concatenate([rows, jnp.zeros((short, L), rows.dtype)], 0)
    return jnp.transpose(rows)


def at(k):
    return slice(k * X, (k + 1) * X)


def beside_after_first(face, h_source, h_inv, low, high, h_line):
    value = low
    forwards = []
    for k in range(D - 1):
        rows = slice(k * 8, (k + 1) * 8)
        value = (h_source[rows, :] + face[k] * value) * h_inv[rows, :]
        forwards.append(value)
    value = high
    h_line[(D - 1) * 8 :, :] = value
    for k in range(D - 2, -1, -1):
        rows = slice(k * 8, (k + 1) * 8)
        value = forwards[k] + (face[k + 1] * h_inv[rows, :]) * value
        h_line[rows, :] = value


def own_after_first(face, source, inv, tint, low, high, v_first):
    value = low
    for k in range(D - 1):
        value = (source[at(k), :] + face[k] * value) * inv[at(k), :]
        v_first[at(k), :] = value
    value = high
    for k in range(D - 1, -1, -1):
        if k < D - 1:
            value = v_first[at(k), :] + (face[k + 1] * inv[at(k), :]) * value
        v_first[at(k), :] = jnp.where(tint == 0, value, 0.0)


def beside_sum(v_first, h_line, column, k, left_core):
    row, lane = iota((X, Y), 0), iota((X, Y), 1)
    lines = v_first[at(k), :]
    sides = h_line[k * 8 : (k + 1) * 8, :]
    lo = jnp.concatenate([sides[XLO0 : XLO0 + 1], sides[XLO1 : XLO1 + 1]], 1)
    hi = jnp.concatenate([sides[XHI : XHI + 1], sides[XHI + 1 : XHI + 2]], 1)

    left = jnp.where(lane == 0, jnp.where(left_core, 0.0, column), pltpu.roll(lines, 1, 1))
    right = jnp.where(
        lane == Y - 1, jnp.where(left_core, column, 0.0), pltpu.roll(lines, Y - 1, 1)
    )
    in_x = jnp.where(row == 0, lo, pltpu.roll(lines, 1, 0)) + jnp.where(
        row == X - 1, hi, pltpu.roll(lines, X - 1, 0)
    )
    return coef_x * in_x + coef_y * (left + right)


def pack_x_kernel(corr, res, state, colour, lo, hi, tint, arrived):
    copies = []
    for out, edge, inner in ((lo, 0, 1), (hi, X - 1, X - 2)):
        for i, (ref, x) in enumerate(((corr, edge), (corr, inner), (res, edge), (state, edge))):
            rows = out.at[pl.ds(i * D, D), :]
            copies.append(pltpu.make_async_copy(ref.at[:, x, :], rows, arrived.at[len(copies)]))
    copies.append(pltpu.make_async_copy(colour, tint, arrived.at[len(copies)]))
    for copy in copies:
        copy.start()
    for copy in copies:
        copy.wait()
    for out, edge in ((lo, 0), (hi, X - 1)):
        row = tint[edge : edge + 1, :].astype(jnp.float32)
        out[4 * D : 4 * D + 8, :] = jnp.broadcast_to(row, (8, Y))


def pack_y_kernel(corr, res, state, colour, out):
    left_core = lax.axis_index("gy") == 0

    def columns(value):
        near = jnp.where(left_core, value[:, L:], value[:, :L])
        return jnp.concatenate([transposed(near[i : i + L]) for i in range(0, near.shape[0], L)], 1)

    def picked(turned, inner):
        return jnp.where(left_core, turned[L - 1 - inner : L - inner], turned[inner : inner + 1])

    field = columns(corr[...])
    out[0:1, :] = picked(field, 0)
    out[1:2, :] = picked(field, 1)
    out[2:3, :] = picked(columns(res[...]), 0)
    out[3:4, :] = picked(columns(state[...]), 0)
    row = picked(columns(colour[...].astype(jnp.float32)), 0)
    out[4:8, :] = jnp.broadcast_to(jnp.concatenate([row, row], 1), (4, Y))


def factor_kernel(level, state, inv, e_first, e_last, k_own, w_x, w_y):
    spacing, face = row_coefficients(level)

    def rows(ref, k):
        return ref[k * X : (k + 1) * X, :]

    ratios, forward = [], []
    ratio = running = None
    for k in range(D - 1):
        pivot = centre_of(spacing[k], face[k], face[k + 1], rows(state, k))
        if k:
            pivot = pivot - face[k] * ratio
        inverse = 1.0 / pivot
        scaled = face[k] * inverse
        running = scaled * running if k else scaled
        ratio = face[k + 1] * inverse
        inv[k * X : (k + 1) * X, :] = inverse
        e_first[k * X : (k + 1) * X, :] = running
    inv[(D - 1) * X :, :] = jnp.zeros((X, Y), jnp.float32)
    e_first[(D - 1) * X :, :] = jnp.zeros((X, Y), jnp.float32)
    e_last[(D - 1) * X :, :] = jnp.ones((X, Y), jnp.float32)
    zero, one = jnp.zeros((X, Y), jnp.float32), jnp.ones((X, Y), jnp.float32)
    first, last = zero, one
    wx = [zero, zero, zero, one * (coef_x * spacing[D - 1])]
    wy = [zero, zero, zero, one * (coef_y * spacing[D - 1])]
    for k in range(D - 2, -1, -1):
        ratio = face[k + 1] * rows(inv, k)
        first = rows(e_first, k) + ratio * first
        last = ratio * last
        e_first[k * X : (k + 1) * X, :] = first
        e_last[k * X : (k + 1) * X, :] = last
        if k == D - 2:
            k_own[X : 2 * X, :] = face[D - 1] * first
            centre = centre_of(spacing[D - 1], face[D - 1], face[D], rows(state, D - 1))
            k_own[2 * X :, :] = centre - face[D - 1] * last
        before = (pltpu.roll(first, 1, 0), pltpu.roll(last, 1, 0))
        after = (pltpu.roll(first, Y - 1, 1), pltpu.roll(last, Y - 1, 1))
        for a, mine in enumerate((first, last)):
            in_x, in_y = (coef_x * spacing[k]) * mine, (coef_y * spacing[k]) * mine
            for b in range(2):
                wx[2 * a + b] = wx[2 * a + b] + in_x * before[b]
                wy[2 * a + b] = wy[2 * a + b] + in_y * after[b]
    k_own[:X, :] = face[0] * first
    for i in range(4):
        w_x[i * X : (i + 1) * X, :] = wx[i]
        w_y[i * X : (i + 1) * X, :] = wy[i]


def interface_kernel(
    level, corr, res, colour, inv, e_first, e_last, k_own, w_x, w_y,
    own_lo, own_hi, got_lo, got_hi, own_y, got_y, cross_lo, cross_hi,
    message, source, h_source, h_inv,
    y_scratch, h_state, h_before, h_first, h_last, h_line, v_first,
):
    spacing, face = row_coefficients(level)
    left_core = lax.axis_index("gy") == 0
    has_lo, has_hi = lax.axis_index("gx") > 0, lax.axis_index("gx") < lax.axis_size("gx") - 1
    row = iota((X, Y), 0)
    lane = iota((X, Y), 1)

    def plane(ref, i):
        return ref[i * D : (i + 1) * D, :]

    def spread(ref):
        for k in range(D):
            at = k % 8 * X
            tile = ref[:, k // 8 * L : (k // 8 + 1) * L]
            y_scratch[k * 8 : (k + 1) * 8, :] = pltpu.roll(tile, L - at, 1) if at else tile
        return [y_scratch[pl.ds(q, D, stride=8), :] for q in range(5)]

    yh_corr, yh_next, yh_res, yh_state, yh_colour = spread(got_y)
    yo_corr, unused, unused, yo_state, unused = spread(own_y)
    yh_colour = yh_colour[0:1]

    small_lane = iota((D, L), 1)

    def corner(ref, there):
        value = jnp.where(left_core, ref[:, 0:1], ref[:, Y - 1 : Y])
        return jnp.where(there, value, 0.0)

    corner_lo, corner_hi = corner(cross_lo, has_lo), corner(cross_hi, has_hi)

    h_state[...] = jnp.zeros_like(h_state)
    h_before[...] = jnp.zeros_like(h_before)

    below = jnp.where(small_lane == 0, corner_lo, pltpu.roll(yh_corr, 1, 1))
    above = jnp.where(small_lane == X - 1, corner_hi, pltpu.roll(yh_corr, L - 1, 1))
    yh_source = yh_res + (coef_x * (below + above) + coef_y * (yo_corr + yh_next))
    h_before[pl.ds(YH, D, stride=8), :] = jnp.where(yh_colour == 0.0, yh_source, 0.0)
    h_state[pl.ds(YH, D, stride=8), :] = yh_state
    h_state[pl.ds(YOWN, D, stride=8), :] = yo_state
    beside_corr = []
    row_k = iota((D, Y), 0)
    lane_k = iota((D, Y), 1)
    for got, own, there, at_corner, places in (
        (got_lo, own_lo, has_lo, corner_lo, (XLO0, XLO1)),
        (got_hi, own_hi, has_hi, corner_hi, (XHI, XHI + 1)),
    ):
        near = jnp.where(there, plane(got, 0), 0.0)
        beside_corr.append(near)
        left = jnp.where(lane_k == 0, jnp.where(left_core, 0.0, at_corner), pltpu.roll(near, 1, 1))
        right = jnp.where(
            lane_k == Y - 1, jnp.where(left_core, at_corner, 0.0), pltpu.roll(near, Y - 1, 1)
        )
        value = plane(got, 2) + (coef_x * (plane(got, 1) + plane(own, 0)) + coef_y * (left + right))
        value = jnp.where(there & (got[4 * D : 4 * D + 1, :] == 0.0), value, 0.0)
        states = plane(got, 3)
        for c, place in enumerate(places):
            h_before[pl.ds(place, D, stride=8), :] = value[:, c * L : (c + 1) * L]
            h_state[pl.ds(place, D, stride=8), :] = states[:, c * L : (c + 1) * L]
    edge_state = plane(own_hi, 3)
    for c in range(2):
        h_state[pl.ds(OWN15 + c, D, stride=8), :] = edge_state[:, c * L : (c + 1) * L]

    def rows8(ref, k):
        return ref[k * 8 : (k + 1) * 8, :]

    ratio = running = None
    inverses, forwards = [], []
    for k in range(D - 1):
        pivot = centre_of(spacing[k], face[k], face[k + 1], rows8(h_state, k))
        if k:
            pivot = pivot - face[k] * ratio
        inverse = 1.0 / pivot
        scaled = face[k] * inverse
        running = scaled * running if k else scaled
        ratio = face[k + 1] * inverse
        inverses.append(inverse)
        forwards.append(running)
        h_inv[k * 8 : (k + 1) * 8, :] = inverse
    h_inv[(D - 1) * 8 :, :] = jnp.zeros((8, L), jnp.float32)
    zero, one = jnp.zeros((8, L), jnp.float32), jnp.ones((8, L), jnp.float32)
    place8 = iota((8, L), 0)
    weight = jnp.where((place8 == YOWN) | (place8 == YH), jnp.float32(coef_y), jnp.float32(coef_x))
    first, last = zero, one
    hw = [zero, zero, zero, weight * spacing[D - 1]]
    hs = spacing[D - 1] * rows8(h_before, D - 1)
    h_source[(D - 1) * 8 :, :] = hs
    hf = [zero, hs]
    hk = [None, None, None]
    h_first[(D - 1) * 8 :, :] = zero
    h_last[(D - 1) * 8 :, :] = one * (coef_x * spacing[D - 1])
    for k in range(D - 2, -1, -1):
        ratio = face[k + 1] * inverses[k]
        first = forwards[k] + ratio * first
        last = ratio * last
        if k == D - 2:
            hk[1] = face[D - 1] * first
            centre = centre_of(spacing[D - 1], face[D - 1], face[D], rows8(h_state, D - 1))
            hk[2] = centre - face[D - 1] * last
        hs = spacing[k] * rows8(h_before, k)
        h_source[k * 8 : (k + 1) * 8, :] = hs
        hf[0] = hf[0] + first * hs
        hf[1] = hf[1] + last * hs
        h_first[k * 8 : (k + 1) * 8, :] = (coef_x * spacing[k]) * first
        h_last[k * 8 : (k + 1) * 8, :] = (coef_x * spacing[k]) * last
        partner = (pltpu.roll(first, 4, 0), pltpu.roll(last, 4, 0))
        for a, mine in enumerate((first, last)):
            mine = (weight * spacing[k]) * mine
            for b in range(2):
                hw[2 * a + b] = hw[2 * a + b] + mine * partner[b]
    hk[0] = face[0] * first

    columns = transposed(
        jnp.concatenate(
            [v[YH : YH + 1] for v in hk + hf] + [v[YOWN : YOWN + 1] for v in hw], 0
        )
    )
    columns_corr = transposed(jnp.concatenate([yh_corr, yh_colour], 0))

    mine = colour[...]
    colour_lo, colour_hi = got_lo[4 * D : 4 * D + 1, :], got_hi[4 * D : 4 * D + 1, :]
    tint = mine.astype(jnp.float32)
    tint_y = columns_corr[:X, D : D + 1]
    at_left, at_right = (lane == 0), (lane == Y - 1)

    def beside_of(value, lo, hi, y_column):
        return (
            jnp.where(row == 0, lo, pltpu.roll(value, 1, 0)),
            jnp.where(row == X - 1, hi, pltpu.roll(value, X - 1, 0)),
            jnp.where(at_left, jnp.where(left_core, 0.0, y_column), pltpu.roll(value, 1, 1)),
            jnp.where(at_right, jnp.where(left_core, y_column, 0.0), pltpu.roll(value, Y - 1, 1)),
        )

    weights = [
        jnp.where((tint == 1.0) & (other == 0.0), 0.0, jnp.float32(amount))
        for other, amount in zip(
            beside_of(tint, colour_lo, colour_hi, tint_y), (coef_x, coef_x, coef_y, coef_y)
        )
    ]
    for k in range(D):
        value = corr[k * X : (k + 1) * X, :]
        around = beside_of(
            value, beside_corr[0][k : k + 1], beside_corr[1][k : k + 1], columns_corr[:X, k : k + 1]
        )
        total = res[k * X : (k + 1) * X, :]
        for w, v in zip(weights, around):
            total = total + w * v
        source[at(k), :] = spacing[k] * total

    beside_after_first(face, h_source, h_inv, zero, zero, h_line)
    still = jnp.zeros((X, Y), jnp.float32)
    own_after_first(face, source, inv, mine, still, still, v_first)
    columns_first = transposed(h_line[pl.ds(YH, D, stride=8), :])
    f_first = f_last = still
    for k in range(D):
        added = beside_sum(v_first, h_line, columns_first[:X, k : k + 1], k, left_core)
        total = source[at(k), :] + jnp.where(mine == 1, spacing[k] * added, 0.0)
        f_first = f_first + e_first[at(k), :] * total
        f_last = f_last + e_last[at(k), :] * total

    def put(r, half, value):
        message[pl.ds(half * R + r, X, stride=2 * R), :] = value

    def put_both(r, value):
        put(r, 0, value[:, :L])
        put(r, 1, value[:, L:])

    short_lane = iota((X, L), 1)
    own_values = [k_own[i * X : (i + 1) * X, :] for i in range(3)] + [f_first, f_last]
    seen_values = own_values[:3] + [jnp.where(tint == 0.0, f, still) for f in own_values[3:]]
    inner_link = [w_y[i * X : (i + 1) * X, :][:, L - 1 : L] for i in (0, 2, 1, 3)]
    for q in range(5):
        own, seen = own_values[q], seen_values[q]
        side = (hk + hf)[q]
        put_both(4 * q, own)
        low = jnp.concatenate([side[XLO0 : XLO0 + 1], side[XLO1 : XLO1 + 1]], 1)
        high = jnp.concatenate([side[XHI : XHI + 1], side[XHI + 1 : XHI + 2]], 1)
        put_both(4 * q + 1, jnp.where(row == 0, low, pltpu.roll(seen, 1, 0)))
        put_both(4 * q + 2, jnp.where(row == X - 1, high, pltpu.roll(seen, X - 1, 0)))
        outer = columns[:X, q : q + 1]
        left_end, right_end = seen[:, L:], seen[:, :L]
        left_none, right_none = (0.0, 0.0) if q >= 3 else (left_end, right_end)
        left_end = jnp.where(
            short_lane == L - 1, jnp.where(left_core, left_none, outer), left_end
        )
        right_end = jnp.where(short_lane == 0, jnp.where(left_core, outer, right_none), right_end)
        if q < 4:
            link = columns[:X, 5 + q : 6 + q]
            left_end = jnp.where(short_lane == L // 2, jnp.where(left_core, 0.0, link), left_end)
            right_end = jnp.where(short_lane == L // 2, inner_link[q], right_end)
        put(4 * q + 3, 0, left_end)
        put(4 * q + 3, 1, right_end)

    edge_first, edge_last = (
        jnp.concatenate([e[k * X : k * X + 1, :] for k in range(D)], 0) for e in (e_first, e_last)
    )
    low_first = jnp.concatenate([h_first[pl.ds(p, D, stride=8), :] for p in (XLO0, XLO1)], 1)
    low_last = jnp.concatenate([h_last[pl.ds(p, D, stride=8), :] for p in (XLO0, XLO1)], 1)
    for a, mine_e in enumerate((edge_first, edge_last)):
        for b, other_e in enumerate((low_first, low_last)):
            i, j = 2 * a + b, 2 * b + a
            edge = jnp.sum(mine_e * other_e, axis=0, keepdims=True)
            put_both(WXM + i, jnp.where(row == 0, edge, w_x[i * X : (i + 1) * X, :]))
            high = jnp.concatenate([hw[i][OWN15 : OWN15 + 1], hw[i][OWN15 + 1 : OWN15 + 2]], 1)
            turned = pltpu.roll(w_x[j * X : (j + 1) * X, :], X - 1, 0)
            put_both(WXP + i, jnp.where(row == X - 1, high, turned))
            link = jnp.where(left_core, columns[:X, 5 + i : 6 + i], 0.0)
            put_both(WYP + i, jnp.where(at_right, link, w_y[i * X : (i + 1) * X, :]))


def separator_kernel(got, colour, out, v_scratch, line_scratch):
    patch = lax.axis_index("gz")
    tint = colour[pl.ds(patch // 2, 1), :]
    tint = jnp.where(patch % 2 == 0, tint[:, :L], tint[:, L:])

    def quantity(q, d):
        return got[d * R + 4 * q : d * R + 4 * q + 4, :]

    off = [quantity(1, d) for d in range(B)]
    diag = [
        quantity(2, d) - quantity(0, d + 1) if d < B - 1 else quantity(2, d) for d in range(B)
    ]
    right = [
        quantity(4, d) + quantity(3, d + 1) if d < B - 1 else quantity(4, d) for d in range(B)
    ]
    middle = B // 2
    up, down = {}, {}
    for n in range(middle):
        d = n
        pivot = diag[d] - off[d] * up[d - 1][1] if n else diag[d]
        inverse = 1.0 / pivot
        up[d] = (inverse, off[d + 1] * inverse)
        d = B - 1 - n
        if d > middle:
            pivot = diag[d] - off[d + 1] * down[d + 1][1] if n else diag[d]
            inverse = 1.0 / pivot
            down[d] = (inverse, off[d] * inverse)
    centre = diag[middle] - off[middle] * up[middle - 1][1] - off[middle + 1] * down[middle + 1][1]
    centre = 1.0 / centre

    def solved(right, sets):
        def cut(value):
            return value[:sets]

        ahead, behind, values = {}, {}, [None] * B
        for n in range(middle):
            d = n
            total = right[d] + cut(off[d]) * ahead[d - 1] if n else right[d]
            ahead[d] = total * cut(up[d][0])
            d = B - 1 - n
            if d > middle:
                total = right[d] + cut(off[d + 1]) * behind[d + 1] if n else right[d]
                behind[d] = total * cut(down[d][0])
        total = (
            right[middle]
            + cut(off[middle]) * ahead[middle - 1]
            + cut(off[middle + 1]) * behind[middle + 1]
        )
        values[middle] = total * cut(centre)
        for n in range(middle):
            d = middle - 1 - n
            values[d] = ahead[d] + cut(up[d][1]) * values[d + 1]
            d = middle + 1 + n
            if d < B:
                values[d] = behind[d] + cut(down[d][1]) * values[d - 1]
        return values

    v_scratch[0:4, :] = jnp.zeros((4, L), jnp.float32)
    for d, value in enumerate(solved(right, 4)):
        v_scratch[4 + d * 4 : 8 + d * 4, :] = value

    lane = iota((B, L), 1)

    def of_set(s):
        return v_scratch[pl.ds(s, B, stride=4), :], v_scratch[pl.ds(4 + s, B, stride=4), :]

    def lines(r):
        return got[pl.ds(r, B, stride=R), :]

    own_pair, lo_pair, hi_pair, end_pair = (of_set(s) for s in range(4))
    first_pair = [jnp.where(tint == 0, v, 0.0) for v in own_pair]
    left_pair = [
        jnp.where(lane == 0, pltpu.roll(e, 1, 1), pltpu.roll(v, 1, 1))
        for e, v in zip(end_pair, first_pair)
    ]
    right_pair = [
        jnp.where(lane == L - 1, pltpu.roll(e, L - 1, 1), pltpu.roll(v, L - 1, 1))
        for e, v in zip(end_pair, first_pair)
    ]
    added = []
    for a in range(2):
        total = jnp.zeros((B, L), jnp.float32)
        for b in range(2):
            i, j = 2 * a + b, 2 * b + a
            total = total + lines(WXM + i) * lo_pair[b]
            total = total + lines(WXP + i) * hi_pair[b]
            total = total + lines(WYP + i) * right_pair[b]
            back = jnp.where(
                lane == 0, pltpu.roll(lines(4 * i + 3), L // 2, 1), pltpu.roll(lines(WYP + j), 1, 1)
            )
            total = total + back * left_pair[b]
        added.append(jnp.where(tint == 1, total, 0.0) + lines(12 + 4 * a))
    line_scratch[0:B, :] = added[0]
    line_scratch[B : B + 8, :] = jnp.zeros((8, L), jnp.float32)
    line_scratch[0:B, :] = added[1] + line_scratch[1 : B + 1, :]
    second = [line_scratch[d : d + 1, :] for d in range(B)]
    values = solved(second, 1)
    line_scratch[0:1, :] = jnp.zeros((1, L), jnp.float32)
    for d in range(B):
        line_scratch[d + 1 : d + 2, :] = values[d]
    results = [line_scratch[0:B, :], line_scratch[1 : B + 1, :]]
    results += [*lo_pair, *hi_pair, *end_pair]
    for i, value in enumerate(results):
        out[pl.ds(i, B, stride=8), :] = value


def finish_kernel(level, source, inv, h_source, h_inv, colour, got, out, v_first, h_line):
    spacing, face = row_coefficients(level)
    left_core = lax.axis_index("gy") == 0
    mine = colour[...]

    def own(i):
        return jnp.concatenate([got[pl.ds(h * 8 + i, X, stride=16), :] for h in range(2)], 1)

    low, high = own(0), own(1)
    ends = []
    for i in (6, 7):
        near = got[pl.ds(8 + i, X, stride=16), :]
        far = pltpu.roll(got[pl.ds(i, X, stride=16), :], 1, 1)
        ends.append(jnp.where(left_core, near, far)[:, 0:1])
    short_lane = iota((X, L), 1)
    pair = jnp.where(short_lane == 0, ends[0], ends[1])
    turned = transposed(pair)
    nothing = jnp.zeros((1, L), jnp.float32)

    def beside(b):
        at = {XHI: 30 * 8 + 4, XHI + 1: 31 * 8 + 4, XLO0: 2, XLO1: 8 + 2}
        rows = [
            turned[b : b + 1]
            if p == YH
            else got[at[p] + b : at[p] + b + 1, :]
            if p in at
            else nothing
            for p in range(8)
        ]
        return jnp.concatenate(rows, 0)

    beside_after_first(face, h_source, h_inv, beside(0), beside(1), h_line)
    columns = transposed(h_line[pl.ds(YH, D, stride=8), :])
    own_after_first(face, source, inv, mine, low, high, v_first)
    value = low
    for k in range(D - 1):
        added = beside_sum(v_first, h_line, columns[:X, k : k + 1], k, left_core)
        value = (source[at(k), :] + spacing[k] * added + face[k] * value) * inv[at(k), :]
        out[at(k), :] = value
    value = high
    for k in range(D - 1, -1, -1):
        if k < D - 1:
            value = out[at(k), :] + (face[k + 1] * inv[at(k), :]) * value
        out[at(k), :] = jnp.where(mine == 0, v_first[at(k), :], value)


VMEM = pl.BlockSpec(memory_space=pltpu.VMEM)
ANY = pl.BlockSpec(memory_space=pl.ANY)
SMEM = pl.BlockSpec(memory_space=pltpu.SMEM)


def f32(*shape):
    return jax.ShapeDtypeStruct(shape, jnp.float32)


def call(kernel, outs, specs, scratch, cost, *args, vmem=32):
    return pl.pallas_call(
        kernel,
        out_shape=outs,
        in_specs=specs,
        out_specs=jax.tree.map(lambda _: VMEM, outs),
        scratch_shapes=[
            pltpu.VMEM(s, jnp.float32) if isinstance(s, tuple) else s for s in scratch
        ],
        compiler_params=pltpu.CompilerParams(vmem_limit_bytes=vmem * 1024 * 1024),
        cost_estimate=pl.CostEstimate(flops=cost, bytes_accessed=cost, transcendentals=0),
    )(*args)


def on_device(correction, residual, state, level, colour):
    corr, res, st = (v.reshape(D * X, Y) for v in (correction, residual, state))
    own_lo, own_hi = call(
        pack_x_kernel, (f32(72, Y), f32(72, Y)), [ANY] * 4,
        [pltpu.VMEM((X, Y), jnp.int32), pltpu.SemaphoreType.DMA((9,))],
        1 << 20, correction, residual, state, colour, vmem=60,
    )
    xs = lax.axis_size("gx")
    ring = [(i, (i + 1) % xs) for i in range(xs)]
    got_lo = lax.ppermute(own_hi, "gx", ring)
    got_hi = lax.ppermute(own_lo, "gx", [(b, a) for a, b in ring])
    own_y = call(
        pack_y_kernel, f32(8, Y), [VMEM] * 4, [], 1 << 20, corr, res, st, colour
    )
    swap = [(0, 1), (1, 0)]
    got_y = lax.ppermute(own_y, "gy", swap)
    field = f32(D * X, Y)
    inv, e_first, e_last, k_own, w_x, w_y = call(
        factor_kernel, (field, field, field, f32(3 * X, Y), f32(4 * X, Y), f32(4 * X, Y)),
        [SMEM, VMEM], [], 1 << 22, level, st,
    )
    got_lo, got_hi, inv, own_y = lax.optimization_barrier((got_lo, got_hi, inv, own_y))
    cross_lo = lax.ppermute(got_lo[:D], "gy", swap)
    cross_hi = lax.ppermute(got_hi[:D], "gy", swap)
    message, source, h_source, h_inv = call(
        interface_kernel, (f32(B * R, L), field, f32(8 * D, L), f32(8 * D, L)),
        [SMEM] + [VMEM] * 17, [(8 * D, L)] * 6 + [(D * X, Y)], 1 << 22,
        level, corr, res, colour, inv, e_first, e_last, k_own, w_x, w_y,
        own_lo, own_hi, got_lo, got_hi, own_y, got_y, cross_lo, cross_hi,
    )

    def exchanged(value, rows):
        blocks = value.reshape(B, rows, L)
        return lax.all_to_all(blocks, "gz", 0, 0, tiled=True).reshape(B * rows, L)

    separators = call(
        separator_kernel, f32(B * 8, L), [VMEM] * 2, [(4 * B + 8, L), (B + 8, L)],
        1 << 21, exchanged(message, R), colour,
    )
    out = call(
        finish_kernel, field, [SMEM] + [VMEM] * 6, [(D * X, Y), (8 * D, L)], 1 << 21,
        level, source, inv, h_source, h_inv, colour, exchanged(separators, 8),
    )
    return out.reshape(D, X, Y)


def solution(mesh):
    block = P("gz", "gx", "gy")
    return jax.shard_map(
        on_device,
        mesh=mesh,
        in_specs=(block, block, block, P(), P("gx", "gy")),
        out_specs=block,
        check_vma=False,
    )
```

```python
import jax
import jax.numpy as jnp
from jax import lax
from jax.experimental import pallas as pl
from jax.experimental.pallas import tpu as pltpu
from jax.sharding import PartitionSpec as P

coef_z = 1000.0
coef_x = 0.3
coef_y = 0.2
bratu_lambda = 0.2

D = 16
X = 16
Y = 256
L = 128
B = 32
R = 16

XHI, YH, XLO0, OWN15, YOWN, XLO1 = 0, 2, 3, 4, 6, 7
PER, HIGH_LINK, LEFT, RIGHT = 18, 90, 96, 112
TURNED = (0, 2, 1, 3)


def iota(shape, dim):
    return lax.broadcasted_iota(jnp.int32, shape, dim)


def row_coefficients(level_ref):
    base = lax.axis_index("gz") * D
    last = level_ref.shape[0] - 1

    def spacing(row):
        level = level_ref[jnp.clip(base + row, 0, last)]
        once = jnp.where((level & 1) == 1, jnp.float32(1.3), jnp.float32(1.0))
        twice = jnp.where((level & 2) == 2, jnp.float32(1.3 * 1.3), jnp.float32(1.0))
        return jnp.float32(0.8) * (once * twice)

    around = [spacing(row) for row in range(-1, D + 1)]
    faces = []
    for i in range(D + 1):
        inside = (base + i > 0) & (base + i <= last)
        face = jnp.float32(coef_z * 2.0) / (around[i] + around[i + 1])
        faces.append(jnp.where(inside, face, jnp.float32(0.0)))
    return around[1 : D + 1], faces


def centre_of(spacing, low, high, state):
    return (low + high) + spacing * ((2.0 * coef_x + 2.0 * coef_y) - bratu_lambda * jnp.exp(state))


def transposed(rows):
    short = L - rows.shape[0]
    if short:
        rows = jnp.concatenate([rows, jnp.zeros((short, L), rows.dtype)], 0)
    return jnp.transpose(rows)


def at(k):
    return slice(k * X, (k + 1) * X)


def beside_after_first(face, h_source, h_inv, low, high, h_line):
    value = low
    forwards = []
    for k in range(D - 1):
        rows = slice(k * 8, (k + 1) * 8)
        value = (h_source[rows, :] + face[k] * value) * h_inv[rows, :]
        forwards.append(value)
    value = high
    h_line[(D - 1) * 8 :, :] = value
    for k in range(D - 2, -1, -1):
        rows = slice(k * 8, (k + 1) * 8)
        value = forwards[k] + (face[k + 1] * h_inv[rows, :]) * value
        h_line[rows, :] = value


def own_after_first(face, source, inv, tint, low, high, v_first):
    value = low
    for k in range(D - 1):
        value = (source[at(k), :] + face[k] * value) * inv[at(k), :]
        v_first[at(k), :] = value
    value = high
    for k in range(D - 1, -1, -1):
        if k < D - 1:
            value = v_first[at(k), :] + (face[k + 1] * inv[at(k), :]) * value
        v_first[at(k), :] = jnp.where(tint == 0, value, 0.0)


def beside_sum(v_first, h_line, column, k, left_core):
    row, lane = iota((X, Y), 0), iota((X, Y), 1)
    lines = v_first[at(k), :]
    sides = h_line[k * 8 : (k + 1) * 8, :]
    lo = jnp.concatenate([sides[XLO0 : XLO0 + 1], sides[XLO1 : XLO1 + 1]], 1)
    hi = jnp.concatenate([sides[XHI : XHI + 1], sides[XHI + 1 : XHI + 2]], 1)

    left = jnp.where(lane == 0, jnp.where(left_core, 0.0, column), pltpu.roll(lines, 1, 1))
    right = jnp.where(
        lane == Y - 1, jnp.where(left_core, column, 0.0), pltpu.roll(lines, Y - 1, 1)
    )
    in_x = jnp.where(row == 0, lo, pltpu.roll(lines, 1, 0)) + jnp.where(
        row == X - 1, hi, pltpu.roll(lines, X - 1, 0)
    )
    return coef_x * in_x + coef_y * (left + right)


def pack_x_kernel(corr, res, state, colour, lo, hi, tint, arrived):
    copies = []
    for out, edge, inner in ((lo, 0, 1), (hi, X - 1, X - 2)):
        for i, (ref, x) in enumerate(((corr, edge), (corr, inner), (res, edge), (state, edge))):
            rows = out.at[pl.ds(i * D, D), :]
            copies.append(pltpu.make_async_copy(ref.at[:, x, :], rows, arrived.at[len(copies)]))
    copies.append(pltpu.make_async_copy(colour, tint, arrived.at[len(copies)]))
    for copy in copies:
        copy.start()
    for copy in copies:
        copy.wait()
    for out, edge in ((lo, 0), (hi, X - 1)):
        row = tint[edge : edge + 1, :].astype(jnp.float32)
        out[4 * D : 4 * D + 8, :] = jnp.broadcast_to(row, (8, Y))


def pack_y_kernel(corr, res, state, colour, out, tint):
    left_core = lax.axis_index("gy") == 0

    def columns(value):
        near = jnp.where(left_core, value[:, L:], value[:, :L])
        return jnp.concatenate([transposed(near[i : i + L]) for i in range(0, near.shape[0], L)], 1)

    def picked(turned, inner):
        return jnp.where(left_core, turned[L - 1 - inner : L - inner], turned[inner : inner + 1])

    field = columns(corr[...])
    out[0:1, :] = picked(field, 0)
    out[1:2, :] = picked(field, 1)
    out[2:3, :] = picked(columns(res[...]), 0)
    out[3:4, :] = picked(columns(state[...]), 0)
    row = picked(columns(colour[...].astype(jnp.float32)), 0)
    out[4:8, :] = jnp.broadcast_to(jnp.concatenate([row, row], 1), (4, Y))
    shifted = jnp.concatenate([jnp.zeros((1, Y), jnp.float32), colour[...].astype(jnp.float32)], 0)
    for c in range(2):
        tint[c * L : (c + 1) * L, :] = transposed(shifted[:, c * L : (c + 1) * L])


def factor_kernel(level, state, inv, e_first, e_last, k_own, w_x, w_y):
    spacing, face = row_coefficients(level)

    def rows(ref, k):
        return ref[k * X : (k + 1) * X, :]

    ratios, forward = [], []
    ratio = running = None
    for k in range(D - 1):
        pivot = centre_of(spacing[k], face[k], face[k + 1], rows(state, k))
        if k:
            pivot = pivot - face[k] * ratio
        inverse = 1.0 / pivot
        scaled = face[k] * inverse
        running = scaled * running if k else scaled
        ratio = face[k + 1] * inverse
        inv[k * X : (k + 1) * X, :] = inverse
        e_first[k * X : (k + 1) * X, :] = running
    inv[(D - 1) * X :, :] = jnp.zeros((X, Y), jnp.float32)
    e_first[(D - 1) * X :, :] = jnp.zeros((X, Y), jnp.float32)
    e_last[(D - 1) * X :, :] = jnp.ones((X, Y), jnp.float32)
    zero, one = jnp.zeros((X, Y), jnp.float32), jnp.ones((X, Y), jnp.float32)
    first, last = zero, one
    wx = [zero, zero, zero, one * (coef_x * spacing[D - 1])]
    wy = [zero, zero, zero, one * (coef_y * spacing[D - 1])]
    for k in range(D - 2, -1, -1):
        ratio = face[k + 1] * rows(inv, k)
        first = rows(e_first, k) + ratio * first
        last = ratio * last
        e_first[k * X : (k + 1) * X, :] = first
        e_last[k * X : (k + 1) * X, :] = last
        if k == D - 2:
            k_own[X : 2 * X, :] = face[D - 1] * first
            centre = centre_of(spacing[D - 1], face[D - 1], face[D], rows(state, D - 1))
            k_own[2 * X :, :] = centre - face[D - 1] * last
        before = (pltpu.roll(first, 1, 0), pltpu.roll(last, 1, 0))
        after = (pltpu.roll(first, Y - 1, 1), pltpu.roll(last, Y - 1, 1))
        for a, mine in enumerate((first, last)):
            in_x, in_y = (coef_x * spacing[k]) * mine, (coef_y * spacing[k]) * mine
            for b in range(2):
                wx[2 * a + b] = wx[2 * a + b] + in_x * before[b]
                wy[2 * a + b] = wy[2 * a + b] + in_y * after[b]
    k_own[:X, :] = face[0] * first
    for i in range(4):
        w_x[i * X : (i + 1) * X, :] = wx[i]
        w_y[i * X : (i + 1) * X, :] = wy[i]


def interface_kernel(
    level, corr, res, colour, inv, e_first, e_last, k_own, w_x, w_y,
    own_lo, own_hi, got_lo, got_hi, own_y, got_y, cross_lo, cross_hi,
    message, source, h_source, h_inv,
    y_scratch, h_state, h_before, h_first, h_last, h_line, v_first, laid,
):
    spacing, face = row_coefficients(level)
    left_core = lax.axis_index("gy") == 0
    has_lo, has_hi = lax.axis_index("gx") > 0, lax.axis_index("gx") < lax.axis_size("gx") - 1
    row = iota((X, Y), 0)
    lane = iota((X, Y), 1)

    def plane(ref, i):
        return ref[i * D : (i + 1) * D, :]

    def spread(ref):
        for k in range(D):
            at = k % 8 * X
            tile = ref[:, k // 8 * L : (k // 8 + 1) * L]
            y_scratch[k * 8 : (k + 1) * 8, :] = pltpu.roll(tile, L - at, 1) if at else tile
        return [y_scratch[pl.ds(q, D, stride=8), :] for q in range(5)]

    yh_corr, yh_next, yh_res, yh_state, yh_colour = spread(got_y)
    yo_corr, unused, unused, yo_state, unused = spread(own_y)
    yh_colour = yh_colour[0:1]

    small_lane = iota((D, L), 1)

    def corner(ref, there):
        value = jnp.where(left_core, ref[:, 0:1], ref[:, Y - 1 : Y])
        return jnp.where(there, value, 0.0)

    corner_lo, corner_hi = corner(cross_lo, has_lo), corner(cross_hi, has_hi)

    h_state[...] = jnp.zeros_like(h_state)
    h_before[...] = jnp.zeros_like(h_before)

    below = jnp.where(small_lane == 0, corner_lo, pltpu.roll(yh_corr, 1, 1))
    above = jnp.where(small_lane == X - 1, corner_hi, pltpu.roll(yh_corr, L - 1, 1))
    yh_source = yh_res + (coef_x * (below + above) + coef_y * (yo_corr + yh_next))
    h_before[pl.ds(YH, D, stride=8), :] = jnp.where(yh_colour == 0.0, yh_source, 0.0)
    h_state[pl.ds(YH, D, stride=8), :] = yh_state
    h_state[pl.ds(YOWN, D, stride=8), :] = yo_state
    beside_corr = []
    row_k = iota((D, Y), 0)
    lane_k = iota((D, Y), 1)
    for got, own, there, at_corner, places in (
        (got_lo, own_lo, has_lo, corner_lo, (XLO0, XLO1)),
        (got_hi, own_hi, has_hi, corner_hi, (XHI, XHI + 1)),
    ):
        near = jnp.where(there, plane(got, 0), 0.0)
        beside_corr.append(near)
        left = jnp.where(lane_k == 0, jnp.where(left_core, 0.0, at_corner), pltpu.roll(near, 1, 1))
        right = jnp.where(
            lane_k == Y - 1, jnp.where(left_core, at_corner, 0.0), pltpu.roll(near, Y - 1, 1)
        )
        value = plane(got, 2) + (coef_x * (plane(got, 1) + plane(own, 0)) + coef_y * (left + right))
        value = jnp.where(there & (got[4 * D : 4 * D + 1, :] == 0.0), value, 0.0)
        states = plane(got, 3)
        for c, place in enumerate(places):
            h_before[pl.ds(place, D, stride=8), :] = value[:, c * L : (c + 1) * L]
            h_state[pl.ds(place, D, stride=8), :] = states[:, c * L : (c + 1) * L]
    edge_state = plane(own_hi, 3)
    for c in range(2):
        h_state[pl.ds(OWN15 + c, D, stride=8), :] = edge_state[:, c * L : (c + 1) * L]

    def rows8(ref, k):
        return ref[k * 8 : (k + 1) * 8, :]

    ratio = running = None
    inverses, forwards = [], []
    for k in range(D - 1):
        pivot = centre_of(spacing[k], face[k], face[k + 1], rows8(h_state, k))
        if k:
            pivot = pivot - face[k] * ratio
        inverse = 1.0 / pivot
        scaled = face[k] * inverse
        running = scaled * running if k else scaled
        ratio = face[k + 1] * inverse
        inverses.append(inverse)
        forwards.append(running)
        h_inv[k * 8 : (k + 1) * 8, :] = inverse
    h_inv[(D - 1) * 8 :, :] = jnp.zeros((8, L), jnp.float32)
    zero, one = jnp.zeros((8, L), jnp.float32), jnp.ones((8, L), jnp.float32)
    place8 = iota((8, L), 0)
    weight = jnp.where((place8 == YOWN) | (place8 == YH), jnp.float32(coef_y), jnp.float32(coef_x))
    first, last = zero, one
    hw = [zero, zero, zero, weight * spacing[D - 1]]
    hs = spacing[D - 1] * rows8(h_before, D - 1)
    h_source[(D - 1) * 8 :, :] = hs
    hf = [zero, hs]
    hk = [None, None, None]
    h_first[(D - 1) * 8 :, :] = zero
    h_last[(D - 1) * 8 :, :] = one * (coef_x * spacing[D - 1])
    for k in range(D - 2, -1, -1):
        ratio = face[k + 1] * inverses[k]
        first = forwards[k] + ratio * first
        last = ratio * last
        if k == D - 2:
            hk[1] = face[D - 1] * first
            centre = centre_of(spacing[D - 1], face[D - 1], face[D], rows8(h_state, D - 1))
            hk[2] = centre - face[D - 1] * last
        hs = spacing[k] * rows8(h_before, k)
        h_source[k * 8 : (k + 1) * 8, :] = hs
        hf[0] = hf[0] + first * hs
        hf[1] = hf[1] + last * hs
        h_first[k * 8 : (k + 1) * 8, :] = (coef_x * spacing[k]) * first
        h_last[k * 8 : (k + 1) * 8, :] = (coef_x * spacing[k]) * last
        partner = (pltpu.roll(first, 4, 0), pltpu.roll(last, 4, 0))
        for a, mine in enumerate((first, last)):
            mine = (weight * spacing[k]) * mine
            for b in range(2):
                hw[2 * a + b] = hw[2 * a + b] + mine * partner[b]
    hk[0] = face[0] * first

    columns = transposed(
        jnp.concatenate(
            [v[YH : YH + 1] for v in hk + hf] + [v[YOWN : YOWN + 1] for v in hw], 0
        )
    )
    columns_corr = transposed(jnp.concatenate([yh_corr, yh_colour], 0))

    mine = colour[...]
    colour_lo, colour_hi = got_lo[4 * D : 4 * D + 1, :], got_hi[4 * D : 4 * D + 1, :]
    tint = mine.astype(jnp.float32)
    tint_y = columns_corr[:X, D : D + 1]
    at_left, at_right = (lane == 0), (lane == Y - 1)

    def beside_of(value, lo, hi, y_column):
        return (
            jnp.where(row == 0, lo, pltpu.roll(value, 1, 0)),
            jnp.where(row == X - 1, hi, pltpu.roll(value, X - 1, 0)),
            jnp.where(at_left, jnp.where(left_core, 0.0, y_column), pltpu.roll(value, 1, 1)),
            jnp.where(at_right, jnp.where(left_core, y_column, 0.0), pltpu.roll(value, Y - 1, 1)),
        )

    weights = [
        jnp.where((tint == 1.0) & (other == 0.0), 0.0, jnp.float32(amount))
        for other, amount in zip(
            beside_of(tint, colour_lo, colour_hi, tint_y), (coef_x, coef_x, coef_y, coef_y)
        )
    ]
    for k in range(D):
        value = corr[k * X : (k + 1) * X, :]
        around = beside_of(
            value, beside_corr[0][k : k + 1], beside_corr[1][k : k + 1], columns_corr[:X, k : k + 1]
        )
        total = res[k * X : (k + 1) * X, :]
        for w, v in zip(weights, around):
            total = total + w * v
        source[at(k), :] = spacing[k] * total

    beside_after_first(face, h_source, h_inv, zero, zero, h_line)
    still = jnp.zeros((X, Y), jnp.float32)
    own_after_first(face, source, inv, mine, still, still, v_first)
    columns_first = transposed(h_line[pl.ds(YH, D, stride=8), :])
    f_first = f_last = still
    for k in range(D):
        added = beside_sum(v_first, h_line, columns_first[:X, k : k + 1], k, left_core)
        total = source[at(k), :] + jnp.where(mine == 1, spacing[k] * added, 0.0)
        f_first = f_first + e_first[at(k), :] * total
        f_last = f_last + e_last[at(k), :] * total

    own_values = [k_own[i * X : (i + 1) * X, :] for i in range(3)] + [f_first, f_last]
    seen_values = own_values[:3] + [jnp.where(tint == 0.0, f, still) for f in own_values[3:]]
    slot = lane & 7
    left_slots = right_slots = still
    for q in range(5):
        side, seen, at_q = (hk + hf)[q], seen_values[q], L + PER * q
        low = jnp.concatenate([side[XLO0 : XLO0 + 1], side[XLO1 : XLO1 + 1]], 1)
        high = jnp.concatenate([side[XHI : XHI + 1], side[XHI + 1 : XHI + 2]], 1)
        laid[at_q : at_q + 1, :] = low
        laid[at_q + 1 : at_q + 1 + X, :] = own_values[q]
        laid[at_q + 1 + X : at_q + 2 + X, :] = high
        outer = columns[:X, q : q + 1]
        nothing = still if q >= 3 else seen
        before = jnp.where(at_right, jnp.where(left_core, nothing, outer), seen)
        behind = jnp.where(at_left, jnp.where(left_core, outer, nothing), seen)
        left_slots = jnp.where(slot == q, pltpu.roll(before, 1 + q, 1), left_slots)
        right_slots = jnp.where(slot == q, pltpu.roll(behind, Y - 8 + q, 1), right_slots)
    for i, j in enumerate(TURNED):
        link = columns[:X, 5 + i : 6 + i]
        along = w_y[i * X : (i + 1) * X, :]
        laid[i * X : (i + 1) * X, :] = jnp.where(
            at_right, jnp.where(left_core, link, along), along
        )
        along = w_y[j * X : (j + 1) * X, :]
        along = jnp.where(at_right, jnp.where(left_core, along, link), along)
        if i < 3:
            left_slots = jnp.where(slot == 5 + i, pltpu.roll(along, 6 + i, 1), left_slots)
        else:
            right_slots = jnp.where(slot == 5, pltpu.roll(along, 6, 1), right_slots)
        high = jnp.concatenate([hw[i][OWN15 : OWN15 + 1], hw[i][OWN15 + 1 : OWN15 + 2]], 1)
        laid[L + HIGH_LINK + i : L + HIGH_LINK + i + 1, :] = high
    laid[L + HIGH_LINK + 4 : L + LEFT, :] = jnp.zeros((LEFT - HIGH_LINK - 4, Y), jnp.float32)
    laid[L + LEFT : L + RIGHT, :] = left_slots
    laid[L + RIGHT :, :] = right_slots

    edge_first, edge_last = (
        jnp.concatenate([e[k * X : k * X + 1, :] for k in range(D)], 0) for e in (e_first, e_last)
    )
    low_first = jnp.concatenate([h_first[pl.ds(p, D, stride=8), :] for p in (XLO0, XLO1)], 1)
    low_last = jnp.concatenate([h_last[pl.ds(p, D, stride=8), :] for p in (XLO0, XLO1)], 1)
    for a, mine_e in enumerate((edge_first, edge_last)):
        for b, other_e in enumerate((low_first, low_last)):
            i = 2 * a + b
            edge = jnp.sum(mine_e * other_e, axis=0, keepdims=True)
            along = w_x[i * X : (i + 1) * X, :]
            laid[(4 + i) * X : (5 + i) * X, :] = jnp.where(row == 0, edge, along)

    for tile in range(2):
        for c in range(2):
            turned = jnp.transpose(laid[tile * L : (tile + 1) * L, c * L : (c + 1) * L])
            for n in range(L // 8):
                first_row = (c * (L // 8) + n) * R + 8 * tile
                message[first_row : first_row + 8, :] = turned[8 * n : 8 * n + 8]


def separator_kernel(got, tints, out):
    patch = lax.axis_index("gz")
    tint = tints[pl.ds(pl.multiple_of(patch * 8, 8), 8), :]
    line, lane = iota((8, L), 0), iota((8, L), 1)

    def rolled(value, amount):
        amount = amount % L
        return pltpu.roll(value, amount, 1) if amount else value

    def couplings(d):
        return got[d * R : d * R + 8, :]

    def values_of(d):
        return got[d * R + 8 : d * R + 16, :]

    quantities = []
    for d in range(B):
        tile = values_of(d)
        ends = [jnp.broadcast_to(got[d * R + 8 + q : d * R + 9 + q, :], (8, L)) for q in range(5)]
        quantities.append(
            [jnp.where(lane >= LEFT, ends[q], rolled(tile, -PER * q)) for q in range(5)]
        )
    off = [quantities[d][1] for d in range(B)]

    def joined(here, above, sign):
        return [
            here[d] + sign * above[d + 1] if d < B - 1 else here[d] for d in range(B)
        ]

    diag = joined([v[2] for v in quantities], [v[0] for v in quantities], -1.0)
    right = joined([v[4] for v in quantities], [v[3] for v in quantities], 1.0)
    middle = B // 2
    up, down = {}, {}
    for n in range(middle):
        d = n
        pivot = diag[d] - off[d] * up[d - 1][1] if n else diag[d]
        inverse = 1.0 / pivot
        up[d] = (inverse, off[d + 1] * inverse)
        d = B - 1 - n
        if d > middle:
            pivot = diag[d] - off[d + 1] * down[d + 1][1] if n else diag[d]
            inverse = 1.0 / pivot
            down[d] = (inverse, off[d] * inverse)
    centre = diag[middle] - off[middle] * up[middle - 1][1] - off[middle + 1] * down[middle + 1][1]
    centre = 1.0 / centre

    def solved(right):
        ahead, behind, values = {}, {}, [None] * B
        for n in range(middle):
            d = n
            total = right[d] + off[d] * ahead[d - 1] if n else right[d]
            ahead[d] = total * up[d][0]
            d = B - 1 - n
            if d > middle:
                total = right[d] + off[d + 1] * behind[d + 1] if n else right[d]
                behind[d] = total * down[d][0]
        total = right[middle] + off[middle] * ahead[middle - 1] + off[middle + 1] * behind[middle + 1]
        values[middle] = total * centre
        for n in range(middle):
            d = middle - 1 - n
            values[d] = ahead[d] + up[d][1] * values[d + 1]
            d = middle + 1 + n
            if d < B:
                values[d] = behind[d] + down[d][1] * values[d - 1]
        return values

    around = []
    for value in solved(right):
        first = jnp.where(tint == 1.0, 0.0, value)
        around.append(
            (
                rolled(first, 1),
                rolled(first, -1),
                jnp.where(line == 0, rolled(value, 1 - LEFT), pltpu.roll(first, 1, 0)),
                jnp.where(line == 7, rolled(value, 1 - RIGHT), pltpu.roll(first, 7, 0)),
            )
        )
    still = jnp.zeros((8, L), jnp.float32)
    added = []
    for d in range(B):
        tile, extra = couplings(d), values_of(d)
        totals = []
        for a in range(2):
            total = still
            for b in range(2):
                i, j = 2 * a + b, 2 * b + a
                here = around[d - 1 + b] if d - 1 + b >= 0 else None
                if here is None:
                    continue
                total = total + rolled(tile, 1 - 64 - 16 * i) * here[0]
                after = jnp.where(
                    lane == X, rolled(extra, X - HIGH_LINK - i), rolled(tile, -64 - 16 * j)
                )
                total = total + after * here[1]
                link = got[d * R + 8 + (5 + i if i < 3 else 5) :, :][:1]
                link = rolled(link, 1 - LEFT if i < 3 else 1 - RIGHT)
                back = jnp.where(line == 0, link, pltpu.roll(rolled(tile, 1 - 16 * j), 1, 0))
                total = total + back * here[2]
                total = total + rolled(tile, 1 - 16 * i) * here[3]
            totals.append(jnp.where(tint == 1.0, total, 0.0))
        added.append(totals)
    second = joined(
        [quantities[d][4] + added[d][1] for d in range(B)],
        [quantities[d][3] + added[d][0] for d in range(B)],
        1.0,
    )
    before = still
    for d, value in enumerate(solved(second)):
        ends = jnp.where(line < 4, value, before)
        out[8 * d : 8 * d + 8, :] = jnp.where(
            lane < 32, value, jnp.where(lane < 64, pltpu.roll(before, 32, 1), ends)
        )
        before = value


def finish_kernel(level, source, inv, h_source, h_inv, colour, got, out, v_first, h_line):
    spacing, face = row_coefficients(level)
    left_core = lax.axis_index("gy") == 0
    mine = colour[...]

    turned = jnp.concatenate([jnp.transpose(got[c * L : (c + 1) * L, :]) for c in range(2)], 1)
    low, high = turned[33 : 33 + X], turned[1 : 1 + X]
    nothing = jnp.zeros((1, L), jnp.float32)

    def beside(b):
        at_b = 0 if b else 32
        near = got[Y - 8 + at_b // 8 : Y - 7 + at_b // 8, :]
        far = got[at_b // 8 : at_b // 8 + 1, :]
        end = jnp.where(left_core, pltpu.roll(near, L - RIGHT, 1), pltpu.roll(far, L - LEFT, 1))
        lo, hi = turned[at_b : at_b + 1], turned[at_b + 1 + X : at_b + 2 + X]
        places = {XHI: hi[:, :L], XHI + 1: hi[:, L:], XLO0: lo[:, :L], XLO1: lo[:, L:], YH: end}
        return jnp.concatenate([places.get(p, nothing) for p in range(8)], 0)

    beside_after_first(face, h_source, h_inv, beside(0), beside(1), h_line)
    columns = transposed(h_line[pl.ds(YH, D, stride=8), :])
    own_after_first(face, source, inv, mine, low, high, v_first)
    value = low
    for k in range(D - 1):
        added = beside_sum(v_first, h_line, columns[:X, k : k + 1], k, left_core)
        value = (source[at(k), :] + spacing[k] * added + face[k] * value) * inv[at(k), :]
        out[at(k), :] = value
    value = high
    for k in range(D - 1, -1, -1):
        if k < D - 1:
            value = out[at(k), :] + (face[k + 1] * inv[at(k), :]) * value
        out[at(k), :] = jnp.where(mine == 0, v_first[at(k), :], value)


VMEM = pl.BlockSpec(memory_space=pltpu.VMEM)
ANY = pl.BlockSpec(memory_space=pl.ANY)
SMEM = pl.BlockSpec(memory_space=pltpu.SMEM)


def f32(*shape):
    return jax.ShapeDtypeStruct(shape, jnp.float32)


def call(kernel, outs, specs, scratch, cost, *args, vmem=32):
    return pl.pallas_call(
        kernel,
        out_shape=outs,
        in_specs=specs,
        out_specs=jax.tree.map(lambda _: VMEM, outs),
        scratch_shapes=[
            pltpu.VMEM(s, jnp.float32) if isinstance(s, tuple) else s for s in scratch
        ],
        compiler_params=pltpu.CompilerParams(vmem_limit_bytes=vmem * 1024 * 1024),
        cost_estimate=pl.CostEstimate(flops=cost, bytes_accessed=cost, transcendentals=0),
    )(*args)


def on_device(correction, residual, state, level, colour):
    corr, res, st = (v.reshape(D * X, Y) for v in (correction, residual, state))
    own_lo, own_hi = call(
        pack_x_kernel, (f32(72, Y), f32(72, Y)), [ANY] * 4,
        [pltpu.VMEM((X, Y), jnp.int32), pltpu.SemaphoreType.DMA((9,))],
        1 << 20, correction, residual, state, colour, vmem=60,
    )
    xs = lax.axis_size("gx")
    ring = [(i, (i + 1) % xs) for i in range(xs)]
    got_lo = lax.ppermute(own_hi, "gx", ring)
    got_hi = lax.ppermute(own_lo, "gx", [(b, a) for a, b in ring])
    own_y, tints = call(
        pack_y_kernel, (f32(8, Y), f32(Y, L)), [VMEM] * 4, [], 1 << 20, corr, res, st, colour
    )
    swap = [(0, 1), (1, 0)]
    got_y = lax.ppermute(own_y, "gy", swap)
    field = f32(D * X, Y)
    inv, e_first, e_last, k_own, w_x, w_y = call(
        factor_kernel, (field, field, field, f32(3 * X, Y), f32(4 * X, Y), f32(4 * X, Y)),
        [SMEM, VMEM], [], 1 << 22, level, st,
    )
    got_lo, got_hi, inv, own_y = lax.optimization_barrier((got_lo, got_hi, inv, own_y))
    cross_lo = lax.ppermute(got_lo[:D], "gy", swap)
    cross_hi = lax.ppermute(got_hi[:D], "gy", swap)
    message, source, h_source, h_inv = call(
        interface_kernel, (f32(B * R, L), field, f32(8 * D, L), f32(8 * D, L)),
        [SMEM] + [VMEM] * 17, [(8 * D, L)] * 6 + [(D * X, Y), (2 * L, Y)], 1 << 22,
        level, corr, res, colour, inv, e_first, e_last, k_own, w_x, w_y,
        own_lo, own_hi, got_lo, got_hi, own_y, got_y, cross_lo, cross_hi,
    )

    def exchanged(value, rows):
        blocks = value.reshape(B, rows, L)
        return lax.all_to_all(blocks, "gz", 0, 0, tiled=True).reshape(B * rows, L)

    separators = call(
        separator_kernel, f32(B * 8, L), [VMEM] * 2, [], 1 << 21, exchanged(message, R), tints
    )
    out = call(
        finish_kernel, field, [SMEM] + [VMEM] * 6, [(D * X, Y), (8 * D, L)], 1 << 21,
        level, source, inv, h_source, h_inv, colour, exchanged(separators, 8),
    )
    return out.reshape(D, X, Y)


def solution(mesh):
    block = P("gz", "gx", "gy")
    return jax.shard_map(
        on_device,
        mesh=mesh,
        in_specs=(block, block, block, P(), P("gx", "gy")),
        out_specs=block,
        check_vma=False,
    )
```

```python
import jax
import jax.numpy as jnp
from jax import lax
from jax.experimental import pallas as pl
from jax.experimental.pallas import tpu as pltpu
from jax.sharding import PartitionSpec as P

coef_z = 1000.0
coef_x = 0.3
coef_y = 0.2
bratu_lambda = 0.2

D = 16
X = 16
Y = 256
L = 128
B = 32
R = 16

XHI, YH, XLO0, OWN15, YOWN, XLO1 = 0, 2, 3, 4, 6, 7
PER, HIGH_LINK, LEFT, RIGHT = 18, 90, 96, 112
TURNED = (0, 2, 1, 3)


def iota(shape, dim):
    return lax.broadcasted_iota(jnp.int32, shape, dim)


def row_coefficients(level_ref):
    base = lax.axis_index("gz") * D
    last = level_ref.shape[0] - 1

    def spacing(row):
        level = level_ref[jnp.clip(base + row, 0, last)]
        once = jnp.where((level & 1) == 1, jnp.float32(1.3), jnp.float32(1.0))
        twice = jnp.where((level & 2) == 2, jnp.float32(1.3 * 1.3), jnp.float32(1.0))
        return jnp.float32(0.8) * (once * twice)

    around = [spacing(row) for row in range(-1, D + 1)]
    faces = []
    for i in range(D + 1):
        inside = (base + i > 0) & (base + i <= last)
        face = jnp.float32(coef_z * 2.0) / (around[i] + around[i + 1])
        faces.append(jnp.where(inside, face, jnp.float32(0.0)))
    return around[1 : D + 1], faces


def coefficient_rows(coef, width):
    return (
        [coef[k : k + 1, :width] for k in range(D)],
        [coef[D + k : D + k + 1, :width] for k in range(D + 1)],
    )


def centre_of(spacing, low, high, state):
    return (low + high) + spacing * ((2.0 * coef_x + 2.0 * coef_y) - bratu_lambda * jnp.exp(state))


def transposed(rows):
    short = L - rows.shape[0]
    if short:
        rows = jnp.concatenate([rows, jnp.zeros((short, L), rows.dtype)], 0)
    return jnp.transpose(rows)


def at(k):
    return slice(k * X, (k + 1) * X)


def beside_after_first(face, h_source, h_inv, low, high, h_line):
    value = low
    forwards = []
    for k in range(D - 1):
        rows = slice(k * 8, (k + 1) * 8)
        value = (h_source[rows, :] + face[k] * value) * h_inv[rows, :]
        forwards.append(value)
    value = high
    h_line[(D - 1) * 8 :, :] = value
    for k in range(D - 2, -1, -1):
        rows = slice(k * 8, (k + 1) * 8)
        value = forwards[k] + (face[k + 1] * h_inv[rows, :]) * value
        h_line[rows, :] = value


def own_after_first(face, source, inv, tint, low, high, v_first):
    value = low
    for k in range(D - 1):
        value = (source[at(k), :] + face[k] * value) * inv[at(k), :]
        v_first[at(k), :] = value
    value = high
    for k in range(D - 1, -1, -1):
        if k < D - 1:
            value = v_first[at(k), :] + (face[k + 1] * inv[at(k), :]) * value
        v_first[at(k), :] = jnp.where(tint == 0, value, 0.0)


def sided(columns):
    left = jnp.full(columns.shape, lax.axis_index("gy"), jnp.int32) == 0
    return jnp.where(left, 0.0, columns), jnp.where(left, columns, 0.0)


def beside_sum(v_first, h_line, columns, k):
    row, lane = iota((X, Y), 0), iota((X, Y), 1)
    lines = v_first[at(k), :]
    sides = h_line[k * 8 : (k + 1) * 8, :]
    lo = jnp.concatenate([sides[XLO0 : XLO0 + 1], sides[XLO1 : XLO1 + 1]], 1)
    hi = jnp.concatenate([sides[XHI : XHI + 1], sides[XHI + 1 : XHI + 2]], 1)

    left_column, right_column = (c[:X, k : k + 1] for c in columns)
    left = jnp.where(lane == 0, left_column, pltpu.roll(lines, 1, 1))
    right = jnp.where(lane == Y - 1, right_column, pltpu.roll(lines, Y - 1, 1))
    in_x = jnp.where(row == 0, lo, pltpu.roll(lines, 1, 0)) + jnp.where(
        row == X - 1, hi, pltpu.roll(lines, X - 1, 0)
    )
    return coef_x * in_x + coef_y * (left + right)


def pack_x_kernel(corr, res, state, colour, lo, hi, tint, arrived):
    copies = []
    for out, edge, inner in ((lo, 0, 1), (hi, X - 1, X - 2)):
        for i, (ref, x) in enumerate(((corr, edge), (corr, inner), (res, edge), (state, edge))):
            rows = out.at[pl.ds(i * D, D), :]
            copies.append(pltpu.make_async_copy(ref.at[:, x, :], rows, arrived.at[len(copies)]))
    copies.append(pltpu.make_async_copy(colour, tint, arrived.at[len(copies)]))
    for copy in copies:
        copy.start()
    for copy in copies:
        copy.wait()
    for out, edge in ((lo, 0), (hi, X - 1)):
        row = tint[edge : edge + 1, :].astype(jnp.float32)
        out[4 * D : 4 * D + 8, :] = jnp.broadcast_to(row, (8, Y))


def pack_y_kernel(corr, res, state, colour, out, tint):
    left_core = lax.axis_index("gy") == 0

    def columns(value):
        near = jnp.where(left_core, value[:, L:], value[:, :L])
        return jnp.concatenate([transposed(near[i : i + L]) for i in range(0, near.shape[0], L)], 1)

    def picked(turned, inner):
        return jnp.where(left_core, turned[L - 1 - inner : L - inner], turned[inner : inner + 1])

    field = columns(corr[...])
    out[0:1, :] = picked(field, 0)
    out[1:2, :] = picked(field, 1)
    out[2:3, :] = picked(columns(res[...]), 0)
    out[3:4, :] = picked(columns(state[...]), 0)
    row = picked(columns(colour[...].astype(jnp.float32)), 0)
    out[4:8, :] = jnp.broadcast_to(jnp.concatenate([row, row], 1), (4, Y))
    shifted = jnp.concatenate([jnp.zeros((1, Y), jnp.float32), colour[...].astype(jnp.float32)], 0)
    for c in range(2):
        tint[c * L : (c + 1) * L, :] = transposed(shifted[:, c * L : (c + 1) * L])


def factor_kernel(level, state, inv, e_first, e_last, k_own, w_x, w_y, coef):
    spacing, face = row_coefficients(level)
    for i, value in enumerate(spacing + face):
        coef[i : i + 1, :] = jnp.full((1, Y), value, jnp.float32)
    for i in range(2 * D + 1, coef.shape[0]):
        coef[i : i + 1, :] = jnp.zeros((1, Y), jnp.float32)

    def rows(ref, k):
        return ref[k * X : (k + 1) * X, :]

    ratios, forward = [], []
    ratio = running = None
    for k in range(D - 1):
        pivot = centre_of(spacing[k], face[k], face[k + 1], rows(state, k))
        if k:
            pivot = pivot - face[k] * ratio
        inverse = 1.0 / pivot
        scaled = face[k] * inverse
        running = scaled * running if k else scaled
        ratio = face[k + 1] * inverse
        inv[k * X : (k + 1) * X, :] = inverse
        e_first[k * X : (k + 1) * X, :] = running
    inv[(D - 1) * X :, :] = jnp.zeros((X, Y), jnp.float32)
    e_first[(D - 1) * X :, :] = jnp.zeros((X, Y), jnp.float32)
    e_last[(D - 1) * X :, :] = jnp.ones((X, Y), jnp.float32)
    zero, one = jnp.zeros((X, Y), jnp.float32), jnp.ones((X, Y), jnp.float32)
    first, last = zero, one
    wx = [zero, zero, zero, one * (coef_x * spacing[D - 1])]
    wy = [zero, zero, zero, one * (coef_y * spacing[D - 1])]
    for k in range(D - 2, -1, -1):
        ratio = face[k + 1] * rows(inv, k)
        first = rows(e_first, k) + ratio * first
        last = ratio * last
        e_first[k * X : (k + 1) * X, :] = first
        e_last[k * X : (k + 1) * X, :] = last
        if k == D - 2:
            k_own[X : 2 * X, :] = face[D - 1] * first
            centre = centre_of(spacing[D - 1], face[D - 1], face[D], rows(state, D - 1))
            k_own[2 * X :, :] = centre - face[D - 1] * last
        before = (pltpu.roll(first, 1, 0), pltpu.roll(last, 1, 0))
        after = (pltpu.roll(first, Y - 1, 1), pltpu.roll(last, Y - 1, 1))
        for a, mine in enumerate((first, last)):
            in_x, in_y = (coef_x * spacing[k]) * mine, (coef_y * spacing[k]) * mine
            for b in range(2):
                wx[2 * a + b] = wx[2 * a + b] + in_x * before[b]
                wy[2 * a + b] = wy[2 * a + b] + in_y * after[b]
    k_own[:X, :] = face[0] * first
    for i in range(4):
        w_x[i * X : (i + 1) * X, :] = wx[i]
        w_y[i * X : (i + 1) * X, :] = wy[i]


def local_kernel(
    coef, corr, res, colour, inv, e_first, e_last, k_own, w_x, w_y,
    own_lo, own_hi, got_lo, got_hi, own_y, got_y,
    source, v_first, h_source, h_inv, h_first, h_last, h_mask, coupled, laid,
    y_scratch, h_state, pairs,
):
    spacing, face = coefficient_rows(coef, Y)
    h_spacing, h_face = coefficient_rows(coef, L)
    has_lo, has_hi = lax.axis_index("gx") > 0, lax.axis_index("gx") < lax.axis_size("gx") - 1
    row = iota((X, Y), 0)
    lane = iota((X, Y), 1)

    def plane(ref, i):
        return ref[i * D : (i + 1) * D, :]

    def spread(ref):
        for k in range(D):
            first = k % 8 * X
            tile = ref[:, k // 8 * L : (k // 8 + 1) * L]
            y_scratch[k * 8 : (k + 1) * 8, :] = pltpu.roll(tile, L - first, 1) if first else tile
        return [y_scratch[pl.ds(q, D, stride=8), :] for q in range(5)]

    yh_corr, yh_next, yh_res, yh_state, yh_colour = spread(got_y)
    yo_corr, unused, unused, yo_state, unused = spread(own_y)
    yh_colour = yh_colour[0:1]

    h_state[...] = jnp.zeros_like(h_state)
    h_source[...] = jnp.zeros_like(h_source)
    h_mask[...] = jnp.zeros_like(h_mask)

    small_lane = iota((D, L), 1)
    below = jnp.where(small_lane == 0, 0.0, pltpu.roll(yh_corr, 1, 1))
    above = jnp.where(small_lane == X - 1, 0.0, pltpu.roll(yh_corr, L - 1, 1))
    yh_source = yh_res + (coef_x * (below + above) + coef_y * (yo_corr + yh_next))
    h_source[pl.ds(YH, D, stride=8), :] = jnp.where(yh_colour == 0.0, yh_source, 0.0)
    h_mask[YH : YH + 1, :] = jnp.where(yh_colour == 0.0, 1.0, 0.0)
    h_state[pl.ds(YH, D, stride=8), :] = yh_state
    h_state[pl.ds(YOWN, D, stride=8), :] = yo_state
    beside_corr = []
    lane_k = iota((D, Y), 1)
    for got, own, there, places in (
        (got_lo, own_lo, has_lo, (XLO0, XLO1)),
        (got_hi, own_hi, has_hi, (XHI, XHI + 1)),
    ):
        near = jnp.where(there, plane(got, 0), 0.0)
        beside_corr.append(near)
        left = jnp.where(lane_k == 0, 0.0, pltpu.roll(near, 1, 1))
        right = jnp.where(lane_k == Y - 1, 0.0, pltpu.roll(near, Y - 1, 1))
        value = plane(got, 2) + (coef_x * (plane(got, 1) + plane(own, 0)) + coef_y * (left + right))
        mask = jnp.where(there & (got[4 * D : 4 * D + 1, :] == 0.0), 1.0, 0.0)
        value = jnp.where(mask == 1.0, value, 0.0)
        states = plane(got, 3)
        for c, place in enumerate(places):
            h_source[pl.ds(place, D, stride=8), :] = value[:, c * L : (c + 1) * L]
            h_mask[place : place + 1, :] = mask[:, c * L : (c + 1) * L]
            h_state[pl.ds(place, D, stride=8), :] = states[:, c * L : (c + 1) * L]
    edge_state = plane(own_hi, 3)
    for c in range(2):
        h_state[pl.ds(OWN15 + c, D, stride=8), :] = edge_state[:, c * L : (c + 1) * L]

    def rows8(ref, k):
        return ref[k * 8 : (k + 1) * 8, :]

    ratio = running = None
    inverses, forwards = [], []
    for k in range(D - 1):
        pivot = centre_of(h_spacing[k], h_face[k], h_face[k + 1], rows8(h_state, k))
        if k:
            pivot = pivot - h_face[k] * ratio
        inverse = 1.0 / pivot
        scaled = h_face[k] * inverse
        running = scaled * running if k else scaled
        ratio = h_face[k + 1] * inverse
        inverses.append(inverse)
        forwards.append(running)
        h_inv[k * 8 : (k + 1) * 8, :] = inverse
    h_inv[(D - 1) * 8 :, :] = jnp.zeros((8, L), jnp.float32)
    zero, one = jnp.zeros((8, L), jnp.float32), jnp.ones((8, L), jnp.float32)
    place8 = iota((8, L), 0)
    weight = jnp.where((place8 == YOWN) | (place8 == YH), jnp.float32(coef_y), jnp.float32(coef_x))
    first, last = zero, one
    hw = [zero, zero, zero, weight * h_spacing[D - 1]]
    h_source[(D - 1) * 8 :, :] = h_spacing[D - 1] * rows8(h_source, D - 1)
    hk = [None, None, None]
    h_first[(D - 1) * 8 :, :] = zero
    h_last[(D - 1) * 8 :, :] = one
    for k in range(D - 2, -1, -1):
        ratio = h_face[k + 1] * inverses[k]
        first = forwards[k] + ratio * first
        last = ratio * last
        if k == D - 2:
            hk[1] = h_face[D - 1] * first
            centre = centre_of(h_spacing[D - 1], h_face[D - 1], h_face[D], rows8(h_state, D - 1))
            hk[2] = centre - h_face[D - 1] * last
        h_source[k * 8 : (k + 1) * 8, :] = h_spacing[k] * rows8(h_source, k)
        h_first[k * 8 : (k + 1) * 8, :] = first
        h_last[k * 8 : (k + 1) * 8, :] = last
        partner = (pltpu.roll(first, 4, 0), pltpu.roll(last, 4, 0))
        for a, mine in enumerate((first, last)):
            mine = (weight * h_spacing[k]) * mine
            for b in range(2):
                hw[2 * a + b] = hw[2 * a + b] + mine * partner[b]
    hk[0] = h_face[0] * first

    columns = transposed(
        jnp.concatenate([v[YH : YH + 1] for v in hk] + [v[YOWN : YOWN + 1] for v in hw], 0)
    )
    columns_corr = sided(transposed(jnp.concatenate([yh_corr, yh_colour], 0)))

    mine = colour[...]
    colour_lo, colour_hi = got_lo[4 * D : 4 * D + 1, :], got_hi[4 * D : 4 * D + 1, :]
    tint = mine.astype(jnp.float32)
    at_left, at_right = (lane == 0), (lane == Y - 1)

    def beside_of(value, lo, hi, k):
        return (
            jnp.where(row == 0, lo, pltpu.roll(value, 1, 0)),
            jnp.where(row == X - 1, hi, pltpu.roll(value, X - 1, 0)),
            jnp.where(at_left, columns_corr[0][:X, k : k + 1], pltpu.roll(value, 1, 1)),
            jnp.where(at_right, columns_corr[1][:X, k : k + 1], pltpu.roll(value, Y - 1, 1)),
        )

    weights = [
        jnp.where((tint == 1.0) & (other == 0.0), 0.0, jnp.float32(amount))
        for other, amount in zip(
            beside_of(tint, colour_lo, colour_hi, D), (coef_x, coef_x, coef_y, coef_y)
        )
    ]
    for k in range(D):
        around = beside_of(
            corr[at(k), :], beside_corr[0][k : k + 1], beside_corr[1][k : k + 1], k
        )
        total = res[at(k), :]
        for w, v in zip(weights, around):
            total = total + w * v
        source[at(k), :] = spacing[k] * total
    still = jnp.zeros((X, Y), jnp.float32)
    own_after_first(face, source, inv, mine, still, still, v_first)

    masks = end_masks()
    slot = lane & 7
    left_slots = right_slots = still
    for q in range(3):
        own = k_own[q * X : (q + 1) * X, :]
        put_lines(laid, q, hk[q], own)
        left, right = end_slots(masks, q, columns[:X, q : q + 1], own, own)
        left_slots = jnp.where(slot == q, left, left_slots)
        right_slots = jnp.where(slot == q, right, right_slots)
    for i, j in enumerate(TURNED):
        link = columns[:X, 3 + i : 4 + i]
        along = w_y[i * X : (i + 1) * X, :]
        pairs[i * X : (i + 1) * X, :] = jnp.where(masks[2], link, along)
        along = jnp.where(masks[1], link, w_y[j * X : (j + 1) * X, :])
        if i < 3:
            left_slots = jnp.where(slot == 5 + i, pltpu.roll(along, 6 + i, 1), left_slots)
        else:
            right_slots = jnp.where(slot == 5, pltpu.roll(along, 6, 1), right_slots)
        high = jnp.concatenate([hw[i][OWN15 : OWN15 + 1], hw[i][OWN15 + 1 : OWN15 + 2]], 1)
        laid[HIGH_LINK + i : HIGH_LINK + i + 1, :] = high
    laid[PER * 3 : PER * 5, :] = jnp.zeros((PER * 2, Y), jnp.float32)
    laid[HIGH_LINK + 4 : LEFT, :] = jnp.zeros((LEFT - HIGH_LINK - 4, Y), jnp.float32)
    laid[LEFT:RIGHT, :] = left_slots
    laid[RIGHT:, :] = right_slots

    amounts = coef_x * coef[0:D, 0:1]
    edges = [
        amounts * jnp.concatenate([e[k * X : k * X + 1, :] for k in range(D)], 0)
        for e in (e_first, e_last)
    ]
    lows = [
        jnp.concatenate([h[pl.ds(p, D, stride=8), :] for p in (XLO0, XLO1)], 1)
        for h in (h_first, h_last)
    ]
    for a in range(2):
        for b in range(2):
            i = 2 * a + b
            edge = jnp.sum(edges[a] * lows[b], axis=0, keepdims=True)
            along = w_x[i * X : (i + 1) * X, :]
            pairs[(4 + i) * X : (5 + i) * X, :] = jnp.where(row == 0, edge, along)
    for c in range(2):
        coupled[c * L : (c + 1) * L, :] = jnp.transpose(pairs[:, c * L : (c + 1) * L])


def end_masks():
    lane = iota((X, Y), 1)
    is_left = jnp.full((X, Y), lax.axis_index("gy"), jnp.int32) == 0
    at_left, at_right = (lane == 0), (lane == Y - 1)
    return at_left & is_left, at_right & ~is_left, at_right & is_left, at_left & ~is_left


def end_slots(masks, q, outer, seen, nothing):
    outer_left, outer_right, none_left, none_right = masks
    before = jnp.where(outer_right, outer, jnp.where(none_left, nothing, seen))
    behind = jnp.where(outer_left, outer, jnp.where(none_right, nothing, seen))
    return pltpu.roll(before, 1 + q, 1), pltpu.roll(behind, Y - 8 + q, 1)


def put_lines(laid, q, side, own):
    low = jnp.concatenate([side[XLO0 : XLO0 + 1], side[XLO1 : XLO1 + 1]], 1)
    high = jnp.concatenate([side[XHI : XHI + 1], side[XHI + 1 : XHI + 2]], 1)
    laid[PER * q : PER * q + 1, :] = low
    laid[PER * q + 1 : PER * q + 1 + X, :] = own
    laid[PER * q + 1 + X : PER * q + 2 + X, :] = high


def message_kernel(
    coef, colour, source, v_first, h_local, h_inv, h_first, h_last, h_mask, coupled, local,
    e_first, e_last, cross_lo, cross_hi,
    message, h_source, h_line, laid,
):
    spacing, face = coefficient_rows(coef, Y)
    h_face = coefficient_rows(coef, L)[1]
    on_left = jnp.where(lax.axis_index("gy") == 0, jnp.float32(1.0), jnp.float32(0.0))
    lane = iota((X, Y), 1)
    small_lane = iota((D, L), 1)
    amounts = coef[0:D, 0:1]
    h_source[...] = h_local[...]
    laid[...] = local[...]

    def add(place, lane_at, value):
        rows = h_source[pl.ds(place, D, stride=8), :]
        rows = rows + jnp.where(small_lane == lane_at, value, 0.0) * h_mask[place : place + 1, :]
        h_source[pl.ds(place, D, stride=8), :] = rows

    xs = lax.axis_size("gx") - 1
    for cross, there, places, lane_at in (
        (cross_lo, lax.axis_index("gx") > 0, (XLO0, XLO1), 0),
        (cross_hi, lax.axis_index("gx") < xs, (XHI, XHI + 1), X - 1),
    ):
        value = on_left * cross[:, 0:1] + (1.0 - on_left) * cross[:, Y - 1 : Y]
        value = amounts * jnp.where(there, value, 0.0)
        add(YH, lane_at, coef_x * value)
        add(places[0], 0, (coef_y * (1.0 - on_left)) * value)
        add(places[1], L - 1, (coef_y * on_left) * value)

    zero = jnp.zeros((8, L), jnp.float32)
    hf = [zero, zero]
    for k in range(D):
        rows = slice(k * 8, (k + 1) * 8)
        hf[0] = hf[0] + h_first[rows, :] * h_source[rows, :]
        hf[1] = hf[1] + h_last[rows, :] * h_source[rows, :]
    columns = transposed(jnp.concatenate([v[YH : YH + 1] for v in hf], 0))

    beside_after_first(h_face, h_source, h_inv, zero, zero, h_line)
    columns_first = sided(transposed(h_line[pl.ds(YH, D, stride=8), :]))
    mine = colour[...]
    still = jnp.zeros((X, Y), jnp.float32)
    f_own = [still, still]
    for k in range(D):
        added = beside_sum(v_first, h_line, columns_first, k)
        total = source[at(k), :] + jnp.where(mine == 1, spacing[k] * added, 0.0)
        f_own[0] = f_own[0] + e_first[at(k), :] * total
        f_own[1] = f_own[1] + e_last[at(k), :] * total

    masks = end_masks()
    slot = lane & 7
    left_slots, right_slots = laid[LEFT:RIGHT, :], laid[RIGHT:, :]
    for i in range(2):
        q = 3 + i
        put_lines(laid, q, hf[i], f_own[i])
        seen = jnp.where(mine == 0, f_own[i], 0.0)
        left, right = end_slots(masks, q, columns[:X, i : i + 1], seen, still)
        left_slots = jnp.where(slot == q, left, left_slots)
        right_slots = jnp.where(slot == q, right, right_slots)
    laid[LEFT:RIGHT, :] = left_slots
    laid[RIGHT:, :] = right_slots
    for c in range(2):
        turned = jnp.transpose(laid[:, c * L : (c + 1) * L])
        for n in range(L // 8):
            p = c * (L // 8) + n
            message[p * R : p * R + 8, :] = coupled[8 * p : 8 * p + 8, :]
            message[p * R + 8 : p * R + 16, :] = turned[8 * n : 8 * n + 8]


def separator_kernel(got, tints, out):
    patch = lax.axis_index("gz")
    tint = tints[pl.ds(pl.multiple_of(patch * 8, 8), 8), :]
    line, lane = iota((8, L), 0), iota((8, L), 1)

    def rolled(value, amount):
        amount = amount % L
        return pltpu.roll(value, amount, 1) if amount else value

    def couplings(d):
        return got[d * R : d * R + 8, :]

    def values_of(d):
        return got[d * R + 8 : d * R + 16, :]

    quantities = []
    for d in range(B):
        tile = values_of(d)
        ends = [jnp.broadcast_to(got[d * R + 8 + q : d * R + 9 + q, :], (8, L)) for q in range(5)]
        quantities.append(
            [jnp.where(lane >= LEFT, ends[q], rolled(tile, -PER * q)) for q in range(5)]
        )
    off = [quantities[d][1] for d in range(B)]

    def joined(here, above, sign):
        return [
            here[d] + sign * above[d + 1] if d < B - 1 else here[d] for d in range(B)
        ]

    diag = joined([v[2] for v in quantities], [v[0] for v in quantities], -1.0)
    right = joined([v[4] for v in quantities], [v[3] for v in quantities], 1.0)
    middle = B // 2
    up, down = {}, {}
    for n in range(middle):
        d = n
        pivot = diag[d] - off[d] * up[d - 1][1] if n else diag[d]
        inverse = 1.0 / pivot
        up[d] = (inverse, off[d + 1] * inverse)
        d = B - 1 - n
        if d > middle:
            pivot = diag[d] - off[d + 1] * down[d + 1][1] if n else diag[d]
            inverse = 1.0 / pivot
            down[d] = (inverse, off[d] * inverse)
    centre = diag[middle] - off[middle] * up[middle - 1][1] - off[middle + 1] * down[middle + 1][1]
    centre = 1.0 / centre

    def solved(right):
        ahead, behind, values = {}, {}, [None] * B
        for n in range(middle):
            d = n
            total = right[d] + off[d] * ahead[d - 1] if n else right[d]
            ahead[d] = total * up[d][0]
            d = B - 1 - n
            if d > middle:
                total = right[d] + off[d + 1] * behind[d + 1] if n else right[d]
                behind[d] = total * down[d][0]
        total = right[middle] + off[middle] * ahead[middle - 1] + off[middle + 1] * behind[middle + 1]
        values[middle] = total * centre
        for n in range(middle):
            d = middle - 1 - n
            values[d] = ahead[d] + up[d][1] * values[d + 1]
            d = middle + 1 + n
            if d < B:
                values[d] = behind[d] + down[d][1] * values[d - 1]
        return values

    around = []
    for value in solved(right):
        first = jnp.where(tint == 1.0, 0.0, value)
        around.append(
            (
                rolled(first, 1),
                rolled(first, -1),
                jnp.where(line == 0, rolled(value, 1 - LEFT), pltpu.roll(first, 1, 0)),
                jnp.where(line == 7, rolled(value, 1 - RIGHT), pltpu.roll(first, 7, 0)),
            )
        )
    still = jnp.zeros((8, L), jnp.float32)
    added = []
    for d in range(B):
        tile, extra = couplings(d), values_of(d)
        totals = []
        for a in range(2):
            total = still
            for b in range(2):
                i, j = 2 * a + b, 2 * b + a
                here = around[d - 1 + b] if d - 1 + b >= 0 else None
                if here is None:
                    continue
                total = total + rolled(tile, 1 - 64 - 16 * i) * here[0]
                after = jnp.where(
                    lane == X, rolled(extra, X - HIGH_LINK - i), rolled(tile, -64 - 16 * j)
                )
                total = total + after * here[1]
                link = got[d * R + 8 + (5 + i if i < 3 else 5) :, :][:1]
                link = rolled(link, 1 - LEFT if i < 3 else 1 - RIGHT)
                back = jnp.where(line == 0, link, pltpu.roll(rolled(tile, 1 - 16 * j), 1, 0))
                total = total + back * here[2]
                total = total + rolled(tile, 1 - 16 * i) * here[3]
            totals.append(jnp.where(tint == 1.0, total, 0.0))
        added.append(totals)
    second = joined(
        [quantities[d][4] + added[d][1] for d in range(B)],
        [quantities[d][3] + added[d][0] for d in range(B)],
        1.0,
    )
    before = still
    for d, value in enumerate(solved(second)):
        ends = jnp.where(line < 4, value, before)
        out[8 * d : 8 * d + 8, :] = jnp.where(
            lane < 32, value, jnp.where(lane < 64, pltpu.roll(before, 32, 1), ends)
        )
        before = value


def finish_kernel(coef, source, inv, h_source, h_inv, colour, got, out, v_first, h_line):
    spacing, face = coefficient_rows(coef, Y)
    h_face = coefficient_rows(coef, L)[1]
    left_core = lax.axis_index("gy") == 0
    mine = colour[...]

    turned = jnp.concatenate([jnp.transpose(got[c * L : (c + 1) * L, :]) for c in range(2)], 1)
    low, high = turned[33 : 33 + X], turned[1 : 1 + X]
    nothing = jnp.zeros((1, L), jnp.float32)

    def beside(b):
        at_b = 0 if b else 32
        near = got[Y - 8 + at_b // 8 : Y - 7 + at_b // 8, :]
        far = got[at_b // 8 : at_b // 8 + 1, :]
        end = jnp.where(left_core, pltpu.roll(near, L - RIGHT, 1), pltpu.roll(far, L - LEFT, 1))
        lo, hi = turned[at_b : at_b + 1], turned[at_b + 1 + X : at_b + 2 + X]
        places = {XHI: hi[:, :L], XHI + 1: hi[:, L:], XLO0: lo[:, :L], XLO1: lo[:, L:], YH: end}
        return jnp.concatenate([places.get(p, nothing) for p in range(8)], 0)

    beside_after_first(h_face, h_source, h_inv, beside(0), beside(1), h_line)
    columns = sided(transposed(h_line[pl.ds(YH, D, stride=8), :]))
    own_after_first(face, source, inv, mine, low, high, v_first)
    value = low
    for k in range(D - 1):
        added = beside_sum(v_first, h_line, columns, k)
        value = (source[at(k), :] + spacing[k] * added + face[k] * value) * inv[at(k), :]
        out[at(k), :] = value
    value = high
    for k in range(D - 1, -1, -1):
        if k < D - 1:
            value = out[at(k), :] + (face[k + 1] * inv[at(k), :]) * value
        out[at(k), :] = jnp.where(mine == 0, v_first[at(k), :], value)


VMEM = pl.BlockSpec(memory_space=pltpu.VMEM)
ANY = pl.BlockSpec(memory_space=pl.ANY)
SMEM = pl.BlockSpec(memory_space=pltpu.SMEM)


def f32(*shape):
    return jax.ShapeDtypeStruct(shape, jnp.float32)


def call(kernel, outs, specs, scratch, cost, *args, vmem=32):
    return pl.pallas_call(
        kernel,
        out_shape=outs,
        in_specs=specs,
        out_specs=jax.tree.map(lambda _: VMEM, outs),
        scratch_shapes=[
            pltpu.VMEM(s, jnp.float32) if isinstance(s, tuple) else s for s in scratch
        ],
        compiler_params=pltpu.CompilerParams(vmem_limit_bytes=vmem * 1024 * 1024),
        cost_estimate=pl.CostEstimate(flops=cost, bytes_accessed=cost, transcendentals=0),
    )(*args)


def on_device(correction, residual, state, level, colour):
    corr, res, st = (v.reshape(D * X, Y) for v in (correction, residual, state))
    own_lo, own_hi = call(
        pack_x_kernel, (f32(72, Y), f32(72, Y)), [ANY] * 4,
        [pltpu.VMEM((X, Y), jnp.int32), pltpu.SemaphoreType.DMA((9,))],
        1 << 20, correction, residual, state, colour, vmem=60,
    )
    xs = lax.axis_size("gx")
    ring = [(i, (i + 1) % xs) for i in range(xs)]
    got_lo = lax.ppermute(own_hi, "gx", ring)
    got_hi = lax.ppermute(own_lo, "gx", [(b, a) for a, b in ring])
    own_y, tints = call(
        pack_y_kernel, (f32(8, Y), f32(Y, L)), [VMEM] * 4, [], 1 << 20, corr, res, st, colour
    )
    swap = [(0, 1), (1, 0)]
    got_y = lax.ppermute(own_y, "gy", swap)
    field = f32(D * X, Y)
    inv, e_first, e_last, k_own, w_x, w_y, coef = call(
        factor_kernel,
        (field, field, field, f32(3 * X, Y), f32(4 * X, Y), f32(4 * X, Y), f32(40, Y)),
        [SMEM, VMEM], [], 1 << 22, level, st,
    )
    got_lo, got_hi, got_y, inv = lax.optimization_barrier((got_lo, got_hi, got_y, inv))
    cross_lo = lax.ppermute(got_lo[:D], "gy", swap)
    cross_hi = lax.ppermute(got_hi[:D], "gy", swap)
    small = f32(8 * D, L)
    source, v_first, h_local, h_inv, h_first, h_last, h_mask, coupled, laid = call(
        local_kernel, (field, field, small, small, small, small, f32(8, L), f32(Y, L), f32(L, Y)),
        [VMEM] * 16, [(8 * D, L), (8 * D, L), (L, Y)], 1 << 22,
        coef, corr, res, colour, inv, e_first, e_last, k_own, w_x, w_y,
        own_lo, own_hi, got_lo, got_hi, own_y, got_y,
    )
    message, h_source = call(
        message_kernel, (f32(B * R, L), small), [VMEM] * 15, [(8 * D, L), (L, Y)], 1 << 22,
        coef, colour, source, v_first, h_local, h_inv, h_first, h_last, h_mask, coupled, laid,
        e_first, e_last, cross_lo, cross_hi,
    )

    def exchanged(value, rows):
        blocks = value.reshape(B, rows, L)
        return lax.all_to_all(blocks, "gz", 0, 0, tiled=True).reshape(B * rows, L)

    separators = call(
        separator_kernel, f32(B * 8, L), [VMEM] * 2, [], 1 << 21, exchanged(message, R), tints
    )
    out = call(
        finish_kernel, field, [VMEM] * 7, [(D * X, Y), (8 * D, L)], 1 << 21,
        coef, source, inv, h_source, h_inv, colour, exchanged(separators, 8),
    )
    return out.reshape(D, X, Y)


def solution(mesh):
    block = P("gz", "gx", "gy")
    return jax.shard_map(
        on_device,
        mesh=mesh,
        in_specs=(block, block, block, P(), P("gx", "gy")),
        out_specs=block,
        check_vma=False,
    )
```

```python
import jax
import jax.numpy as jnp
from jax import lax
from jax.experimental import pallas as pl
from jax.experimental.pallas import tpu as pltpu
from jax.sharding import PartitionSpec as P

coef_z = 1000.0
coef_x = 0.3
coef_y = 0.2
bratu_lambda = 0.2

D = 16
X = 16
Y = 256
L = 128
B = 32
R = 16

XHI, YH, XLO0, OWN15, YOWN, XLO1 = 0, 2, 3, 4, 6, 7
PER, HIGH_LINK, LEFT, RIGHT = 18, 90, 96, 112
TURNED = (0, 2, 1, 3)


def iota(shape, dim):
    return lax.broadcasted_iota(jnp.int32, shape, dim)


def row_coefficients(level_ref):
    base = lax.axis_index("gz") * D
    last = level_ref.shape[0] - 1

    def spacing(row):
        level = level_ref[jnp.clip(base + row, 0, last)]
        once = jnp.where((level & 1) == 1, jnp.float32(1.3), jnp.float32(1.0))
        twice = jnp.where((level & 2) == 2, jnp.float32(1.3 * 1.3), jnp.float32(1.0))
        return jnp.float32(0.8) * (once * twice)

    around = [spacing(row) for row in range(-1, D + 1)]
    faces = []
    for i in range(D + 1):
        inside = (base + i > 0) & (base + i <= last)
        face = jnp.float32(coef_z * 2.0) / (around[i] + around[i + 1])
        faces.append(jnp.where(inside, face, jnp.float32(0.0)))
    return around[1 : D + 1], faces


def coefficient_rows(coef, width):
    return (
        [coef[k : k + 1, :width] for k in range(D)],
        [coef[D + k : D + k + 1, :width] for k in range(D + 1)],
    )


def centre_of(spacing, low, high, state):
    return (low + high) + spacing * ((2.0 * coef_x + 2.0 * coef_y) - bratu_lambda * jnp.exp(state))


def transposed(rows):
    short = L - rows.shape[0]
    if short:
        rows = jnp.concatenate([rows, jnp.zeros((short, L), rows.dtype)], 0)
    return jnp.transpose(rows)


def at(k):
    return slice(k * X, (k + 1) * X)


def beside_after_first(face, h_source, h_inv, low, high, h_line):
    value = low
    forwards = []
    for k in range(D - 1):
        rows = slice(k * 8, (k + 1) * 8)
        value = (h_source[rows, :] + face[k] * value) * h_inv[rows, :]
        forwards.append(value)
    value = high
    h_line[(D - 1) * 8 :, :] = value
    for k in range(D - 2, -1, -1):
        rows = slice(k * 8, (k + 1) * 8)
        value = forwards[k] + (face[k + 1] * h_inv[rows, :]) * value
        h_line[rows, :] = value


def own_after_first(face, source, inv, tint, low, high, v_first):
    value = low
    for k in range(D - 1):
        value = (source[at(k), :] + face[k] * value) * inv[at(k), :]
        v_first[at(k), :] = value
    value = high
    for k in range(D - 1, -1, -1):
        if k < D - 1:
            value = v_first[at(k), :] + (face[k + 1] * inv[at(k), :]) * value
        v_first[at(k), :] = jnp.where(tint == 0, value, 0.0)


def sided(columns):
    left = jnp.full(columns.shape, lax.axis_index("gy"), jnp.int32) == 0
    return jnp.where(left, 0.0, columns), jnp.where(left, columns, 0.0)


def beside_sum(v_first, h_line, columns, k):
    row, lane = iota((X, Y), 0), iota((X, Y), 1)
    lines = v_first[at(k), :]
    sides = h_line[k * 8 : (k + 1) * 8, :]
    lo = jnp.concatenate([sides[XLO0 : XLO0 + 1], sides[XLO1 : XLO1 + 1]], 1)
    hi = jnp.concatenate([sides[XHI : XHI + 1], sides[XHI + 1 : XHI + 2]], 1)

    left_column, right_column = (c[:X, k : k + 1] for c in columns)
    left = jnp.where(lane == 0, left_column, pltpu.roll(lines, 1, 1))
    right = jnp.where(lane == Y - 1, right_column, pltpu.roll(lines, Y - 1, 1))
    in_x = jnp.where(row == 0, lo, pltpu.roll(lines, 1, 0)) + jnp.where(
        row == X - 1, hi, pltpu.roll(lines, X - 1, 0)
    )
    return coef_x * in_x + coef_y * (left + right)


def pack_x_kernel(corr, res, state, colour, lo, hi, tint, arrived):
    copies = []
    for out, edge, inner in ((lo, 0, 1), (hi, X - 1, X - 2)):
        for i, (ref, x) in enumerate(((corr, edge), (corr, inner), (res, edge), (state, edge))):
            rows = out.at[pl.ds(i * D, D), :]
            copies.append(pltpu.make_async_copy(ref.at[:, x, :], rows, arrived.at[len(copies)]))
    copies.append(pltpu.make_async_copy(colour, tint, arrived.at[len(copies)]))
    for copy in copies:
        copy.start()
    for copy in copies:
        copy.wait()
    for out, edge in ((lo, 0), (hi, X - 1)):
        row = tint[edge : edge + 1, :].astype(jnp.float32)
        out[4 * D : 4 * D + 8, :] = jnp.broadcast_to(row, (8, Y))


def pack_y_kernel(corr, res, state, colour, out, tint):
    left_core = lax.axis_index("gy") == 0

    def columns(value):
        near = jnp.where(left_core, value[:, L:], value[:, :L])
        return jnp.concatenate([transposed(near[i : i + L]) for i in range(0, near.shape[0], L)], 1)

    def picked(turned, inner):
        return jnp.where(left_core, turned[L - 1 - inner : L - inner], turned[inner : inner + 1])

    field = columns(corr[...])
    out[0:1, :] = picked(field, 0)
    out[1:2, :] = picked(field, 1)
    out[2:3, :] = picked(columns(res[...]), 0)
    out[3:4, :] = picked(columns(state[...]), 0)
    row = picked(columns(colour[...].astype(jnp.float32)), 0)
    out[4:8, :] = jnp.broadcast_to(jnp.concatenate([row, row], 1), (4, Y))
    shifted = jnp.concatenate([jnp.zeros((1, Y), jnp.float32), colour[...].astype(jnp.float32)], 0)
    for c in range(2):
        tint[c * L : (c + 1) * L, :] = transposed(shifted[:, c * L : (c + 1) * L])


def factor_kernel(level, state, inv, e_first, e_last, k_own, w_x, w_y, coef):
    spacing, face = row_coefficients(level)
    for i, value in enumerate(spacing + face):
        coef[i : i + 1, :] = jnp.full((1, Y), value, jnp.float32)
    for i in range(2 * D + 1, coef.shape[0]):
        coef[i : i + 1, :] = jnp.zeros((1, Y), jnp.float32)

    def rows(ref, k):
        return ref[k * X : (k + 1) * X, :]

    ratios, forward = [], []
    ratio = running = None
    for k in range(D - 1):
        pivot = centre_of(spacing[k], face[k], face[k + 1], rows(state, k))
        if k:
            pivot = pivot - face[k] * ratio
        inverse = 1.0 / pivot
        scaled = face[k] * inverse
        running = scaled * running if k else scaled
        ratio = face[k + 1] * inverse
        inv[k * X : (k + 1) * X, :] = inverse
        e_first[k * X : (k + 1) * X, :] = running
    inv[(D - 1) * X :, :] = jnp.zeros((X, Y), jnp.float32)
    e_first[(D - 1) * X :, :] = jnp.zeros((X, Y), jnp.float32)
    e_last[(D - 1) * X :, :] = jnp.ones((X, Y), jnp.float32)
    zero, one = jnp.zeros((X, Y), jnp.float32), jnp.ones((X, Y), jnp.float32)
    first, last = zero, one
    wx = [zero, zero, zero, one * (coef_x * spacing[D - 1])]
    wy = [zero, zero, zero, one * (coef_y * spacing[D - 1])]
    for k in range(D - 2, -1, -1):
        ratio = face[k + 1] * rows(inv, k)
        first = rows(e_first, k) + ratio * first
        last = ratio * last
        e_first[k * X : (k + 1) * X, :] = first
        e_last[k * X : (k + 1) * X, :] = last
        if k == D - 2:
            k_own[X : 2 * X, :] = face[D - 1] * first
            centre = centre_of(spacing[D - 1], face[D - 1], face[D], rows(state, D - 1))
            k_own[2 * X :, :] = centre - face[D - 1] * last
        before = (pltpu.roll(first, 1, 0), pltpu.roll(last, 1, 0))
        after = (pltpu.roll(first, Y - 1, 1), pltpu.roll(last, Y - 1, 1))
        for a, mine in enumerate((first, last)):
            in_x, in_y = (coef_x * spacing[k]) * mine, (coef_y * spacing[k]) * mine
            for b in range(2):
                wx[2 * a + b] = wx[2 * a + b] + in_x * before[b]
                wy[2 * a + b] = wy[2 * a + b] + in_y * after[b]
    k_own[:X, :] = face[0] * first
    for i in range(4):
        w_x[i * X : (i + 1) * X, :] = wx[i]
        w_y[i * X : (i + 1) * X, :] = wy[i]


def local_kernel(
    coef, corr, res, colour, inv, e_first, e_last, k_own, w_x, w_y,
    own_lo, own_hi, got_lo, got_hi, own_y, got_y,
    source, v_first, h_source, h_inv, h_first, h_last, h_mask, coupled, laid,
    y_scratch, h_state, pairs,
):
    spacing, face = coefficient_rows(coef, Y)
    h_spacing, h_face = coefficient_rows(coef, L)
    has_lo, has_hi = lax.axis_index("gx") > 0, lax.axis_index("gx") < lax.axis_size("gx") - 1
    row = iota((X, Y), 0)
    lane = iota((X, Y), 1)

    def plane(ref, i):
        return ref[i * D : (i + 1) * D, :]

    def spread(ref):
        for k in range(D):
            first = k % 8 * X
            tile = ref[:, k // 8 * L : (k // 8 + 1) * L]
            y_scratch[k * 8 : (k + 1) * 8, :] = pltpu.roll(tile, L - first, 1) if first else tile
        return [y_scratch[pl.ds(q, D, stride=8), :] for q in range(5)]

    yh_corr, yh_next, yh_res, yh_state, yh_colour = spread(got_y)
    yo_corr, unused, unused, yo_state, unused = spread(own_y)
    yh_colour = yh_colour[0:1]

    h_state[...] = jnp.zeros_like(h_state)
    h_source[...] = jnp.zeros_like(h_source)
    h_mask[...] = jnp.zeros_like(h_mask)

    small_lane = iota((D, L), 1)
    below = jnp.where(small_lane == 0, 0.0, pltpu.roll(yh_corr, 1, 1))
    above = jnp.where(small_lane == X - 1, 0.0, pltpu.roll(yh_corr, L - 1, 1))
    yh_source = yh_res + (coef_x * (below + above) + coef_y * (yo_corr + yh_next))
    h_source[pl.ds(YH, D, stride=8), :] = jnp.where(yh_colour == 0.0, yh_source, 0.0)
    h_mask[YH : YH + 1, :] = jnp.where(yh_colour == 0.0, 1.0, 0.0)
    h_state[pl.ds(YH, D, stride=8), :] = yh_state
    h_state[pl.ds(YOWN, D, stride=8), :] = yo_state
    beside_corr = []
    lane_k = iota((D, Y), 1)
    for got, own, there, places in (
        (got_lo, own_lo, has_lo, (XLO0, XLO1)),
        (got_hi, own_hi, has_hi, (XHI, XHI + 1)),
    ):
        near = jnp.where(there, plane(got, 0), 0.0)
        beside_corr.append(near)
        left = jnp.where(lane_k == 0, 0.0, pltpu.roll(near, 1, 1))
        right = jnp.where(lane_k == Y - 1, 0.0, pltpu.roll(near, Y - 1, 1))
        value = plane(got, 2) + (coef_x * (plane(got, 1) + plane(own, 0)) + coef_y * (left + right))
        mask = jnp.where(there & (got[4 * D : 4 * D + 1, :] == 0.0), 1.0, 0.0)
        value = jnp.where(mask == 1.0, value, 0.0)
        states = plane(got, 3)
        for c, place in enumerate(places):
            h_source[pl.ds(place, D, stride=8), :] = value[:, c * L : (c + 1) * L]
            h_mask[place : place + 1, :] = mask[:, c * L : (c + 1) * L]
            h_state[pl.ds(place, D, stride=8), :] = states[:, c * L : (c + 1) * L]
    edge_state = plane(own_hi, 3)
    for c in range(2):
        h_state[pl.ds(OWN15 + c, D, stride=8), :] = edge_state[:, c * L : (c + 1) * L]

    def rows8(ref, k):
        return ref[k * 8 : (k + 1) * 8, :]

    ratio = running = None
    inverses, forwards = [], []
    for k in range(D - 1):
        pivot = centre_of(h_spacing[k], h_face[k], h_face[k + 1], rows8(h_state, k))
        if k:
            pivot = pivot - h_face[k] * ratio
        inverse = 1.0 / pivot
        scaled = h_face[k] * inverse
        running = scaled * running if k else scaled
        ratio = h_face[k + 1] * inverse
        inverses.append(inverse)
        forwards.append(running)
        h_inv[k * 8 : (k + 1) * 8, :] = inverse
    h_inv[(D - 1) * 8 :, :] = jnp.zeros((8, L), jnp.float32)
    zero, one = jnp.zeros((8, L), jnp.float32), jnp.ones((8, L), jnp.float32)
    place8 = iota((8, L), 0)
    weight = jnp.where((place8 == YOWN) | (place8 == YH), jnp.float32(coef_y), jnp.float32(coef_x))
    first, last = zero, one
    hw = [zero, zero, zero, weight * h_spacing[D - 1]]
    h_source[(D - 1) * 8 :, :] = h_spacing[D - 1] * rows8(h_source, D - 1)
    hk = [None, None, None]
    h_first[(D - 1) * 8 :, :] = zero
    h_last[(D - 1) * 8 :, :] = one
    for k in range(D - 2, -1, -1):
        ratio = h_face[k + 1] * inverses[k]
        first = forwards[k] + ratio * first
        last = ratio * last
        if k == D - 2:
            hk[1] = h_face[D - 1] * first
            centre = centre_of(h_spacing[D - 1], h_face[D - 1], h_face[D], rows8(h_state, D - 1))
            hk[2] = centre - h_face[D - 1] * last
        h_source[k * 8 : (k + 1) * 8, :] = h_spacing[k] * rows8(h_source, k)
        h_first[k * 8 : (k + 1) * 8, :] = first
        h_last[k * 8 : (k + 1) * 8, :] = last
        partner = (pltpu.roll(first, 4, 0), pltpu.roll(last, 4, 0))
        for a, mine in enumerate((first, last)):
            mine = (weight * h_spacing[k]) * mine
            for b in range(2):
                hw[2 * a + b] = hw[2 * a + b] + mine * partner[b]
    hk[0] = h_face[0] * first

    columns = transposed(
        jnp.concatenate([v[YH : YH + 1] for v in hk] + [v[YOWN : YOWN + 1] for v in hw], 0)
    )
    columns_corr = sided(transposed(jnp.concatenate([yh_corr, yh_colour], 0)))

    mine = colour[...]
    colour_lo, colour_hi = got_lo[4 * D : 4 * D + 1, :], got_hi[4 * D : 4 * D + 1, :]
    tint = mine.astype(jnp.float32)
    at_left, at_right = (lane == 0), (lane == Y - 1)

    def beside_of(value, lo, hi, k):
        return (
            jnp.where(row == 0, lo, pltpu.roll(value, 1, 0)),
            jnp.where(row == X - 1, hi, pltpu.roll(value, X - 1, 0)),
            jnp.where(at_left, columns_corr[0][:X, k : k + 1], pltpu.roll(value, 1, 1)),
            jnp.where(at_right, columns_corr[1][:X, k : k + 1], pltpu.roll(value, Y - 1, 1)),
        )

    weights = [
        jnp.where((tint == 1.0) & (other == 0.0), 0.0, jnp.float32(amount))
        for other, amount in zip(
            beside_of(tint, colour_lo, colour_hi, D), (coef_x, coef_x, coef_y, coef_y)
        )
    ]
    for k in range(D):
        around = beside_of(
            corr[at(k), :], beside_corr[0][k : k + 1], beside_corr[1][k : k + 1], k
        )
        total = res[at(k), :]
        for w, v in zip(weights, around):
            total = total + w * v
        source[at(k), :] = spacing[k] * total
    still = jnp.zeros((X, Y), jnp.float32)
    own_after_first(face, source, inv, mine, still, still, v_first)

    masks = end_masks()
    slot = lane & 7
    left_slots = right_slots = still
    for q in range(3):
        own = k_own[q * X : (q + 1) * X, :]
        put_lines(laid, q, hk[q], own)
        left, right = end_slots(masks, q, columns[:X, q : q + 1], own, own)
        left_slots = jnp.where(slot == q, left, left_slots)
        right_slots = jnp.where(slot == q, right, right_slots)
    for i, j in enumerate(TURNED):
        link = columns[:X, 3 + i : 4 + i]
        along = w_y[i * X : (i + 1) * X, :]
        pairs[i * X : (i + 1) * X, :] = jnp.where(masks[2], link, along)
        along = jnp.where(masks[1], link, w_y[j * X : (j + 1) * X, :])
        if i < 3:
            left_slots = jnp.where(slot == 5 + i, pltpu.roll(along, 6 + i, 1), left_slots)
        else:
            right_slots = jnp.where(slot == 5, pltpu.roll(along, 6, 1), right_slots)
        high = jnp.concatenate([hw[i][OWN15 : OWN15 + 1], hw[i][OWN15 + 1 : OWN15 + 2]], 1)
        laid[HIGH_LINK + i : HIGH_LINK + i + 1, :] = high
    laid[PER * 3 : PER * 5, :] = jnp.zeros((PER * 2, Y), jnp.float32)
    laid[HIGH_LINK + 4 : LEFT, :] = jnp.zeros((LEFT - HIGH_LINK - 4, Y), jnp.float32)
    laid[LEFT:RIGHT, :] = left_slots
    laid[RIGHT:, :] = right_slots

    amounts = coef_x * coef[0:D, 0:1]
    edges = [
        amounts * jnp.concatenate([e[k * X : k * X + 1, :] for k in range(D)], 0)
        for e in (e_first, e_last)
    ]
    lows = [
        jnp.concatenate([h[pl.ds(p, D, stride=8), :] for p in (XLO0, XLO1)], 1)
        for h in (h_first, h_last)
    ]
    for a in range(2):
        for b in range(2):
            i = 2 * a + b
            edge = jnp.sum(edges[a] * lows[b], axis=0, keepdims=True)
            along = w_x[i * X : (i + 1) * X, :]
            pairs[(4 + i) * X : (5 + i) * X, :] = jnp.where(row == 0, edge, along)
    for c in range(2):
        coupled[c * L : (c + 1) * L, :] = jnp.transpose(pairs[:, c * L : (c + 1) * L])


def end_masks():
    lane = iota((X, Y), 1)
    is_left = jnp.full((X, Y), lax.axis_index("gy"), jnp.int32) == 0
    at_left, at_right = (lane == 0), (lane == Y - 1)
    return at_left & is_left, at_right & ~is_left, at_right & is_left, at_left & ~is_left


def end_slots(masks, q, outer, seen, nothing):
    outer_left, outer_right, none_left, none_right = masks
    before = jnp.where(outer_right, outer, jnp.where(none_left, nothing, seen))
    behind = jnp.where(outer_left, outer, jnp.where(none_right, nothing, seen))
    return pltpu.roll(before, 1 + q, 1), pltpu.roll(behind, Y - 8 + q, 1)


def put_lines(laid, q, side, own):
    low = jnp.concatenate([side[XLO0 : XLO0 + 1], side[XLO1 : XLO1 + 1]], 1)
    high = jnp.concatenate([side[XHI : XHI + 1], side[XHI + 1 : XHI + 2]], 1)
    laid[PER * q : PER * q + 1, :] = low
    laid[PER * q + 1 : PER * q + 1 + X, :] = own
    laid[PER * q + 1 + X : PER * q + 2 + X, :] = high


def message_kernel(
    coef, colour, source, v_first, h_local, h_inv, h_first, h_last, h_mask, coupled, local,
    e_first, e_last, cross_lo, cross_hi,
    message, h_source, h_line, laid,
):
    spacing, face = coefficient_rows(coef, Y)
    h_face = coefficient_rows(coef, L)[1]
    on_left = jnp.where(lax.axis_index("gy") == 0, jnp.float32(1.0), jnp.float32(0.0))
    lane = iota((X, Y), 1)
    small_lane = iota((D, L), 1)
    amounts = coef[0:D, 0:1]
    h_source[...] = h_local[...]
    laid[...] = local[...]

    def add(place, lane_at, value):
        rows = h_source[pl.ds(place, D, stride=8), :]
        rows = rows + jnp.where(small_lane == lane_at, value, 0.0) * h_mask[place : place + 1, :]
        h_source[pl.ds(place, D, stride=8), :] = rows

    xs = lax.axis_size("gx") - 1
    for cross, there, places, lane_at in (
        (cross_lo, lax.axis_index("gx") > 0, (XLO0, XLO1), 0),
        (cross_hi, lax.axis_index("gx") < xs, (XHI, XHI + 1), X - 1),
    ):
        value = on_left * cross[:, 0:1] + (1.0 - on_left) * cross[:, Y - 1 : Y]
        value = amounts * jnp.where(there, value, 0.0)
        add(YH, lane_at, coef_x * value)
        add(places[0], 0, (coef_y * (1.0 - on_left)) * value)
        add(places[1], L - 1, (coef_y * on_left) * value)

    zero = jnp.zeros((8, L), jnp.float32)
    hf = [zero, zero]
    for k in range(D):
        rows = slice(k * 8, (k + 1) * 8)
        hf[0] = hf[0] + h_first[rows, :] * h_source[rows, :]
        hf[1] = hf[1] + h_last[rows, :] * h_source[rows, :]
    columns = transposed(jnp.concatenate([v[YH : YH + 1] for v in hf], 0))

    beside_after_first(h_face, h_source, h_inv, zero, zero, h_line)
    columns_first = sided(transposed(h_line[pl.ds(YH, D, stride=8), :]))
    mine = colour[...]
    still = jnp.zeros((X, Y), jnp.float32)
    f_own = [still, still]
    for k in range(D):
        added = beside_sum(v_first, h_line, columns_first, k)
        total = source[at(k), :] + jnp.where(mine == 1, spacing[k] * added, 0.0)
        f_own[0] = f_own[0] + e_first[at(k), :] * total
        f_own[1] = f_own[1] + e_last[at(k), :] * total

    masks = end_masks()
    slot = lane & 7
    left_slots, right_slots = laid[LEFT:RIGHT, :], laid[RIGHT:, :]
    for i in range(2):
        q = 3 + i
        put_lines(laid, q, hf[i], f_own[i])
        seen = jnp.where(mine == 0, f_own[i], 0.0)
        left, right = end_slots(masks, q, columns[:X, i : i + 1], seen, still)
        left_slots = jnp.where(slot == q, left, left_slots)
        right_slots = jnp.where(slot == q, right, right_slots)
    laid[LEFT:RIGHT, :] = left_slots
    laid[RIGHT:, :] = right_slots
    for c in range(2):
        turned = jnp.transpose(laid[:, c * L : (c + 1) * L])
        for n in range(L // 8):
            p = c * (L // 8) + n
            message[p * R : p * R + 8, :] = coupled[8 * p : 8 * p + 8, :]
            message[p * R + 8 : p * R + 16, :] = turned[8 * n : 8 * n + 8]


def separator_kernel(got, tints, out, ends):
    patch = lax.axis_index("gz")
    tint = tints[pl.ds(pl.multiple_of(patch * 8, 8), 8), :]
    line, lane = iota((8, L), 0), iota((8, L), 1)

    def rolled(value, amount):
        amount = amount % L
        return pltpu.roll(value, amount, 1) if amount else value

    def couplings(d):
        return got[d * R : d * R + 8, :]

    def values_of(d):
        return got[d * R + 8 : d * R + 16, :]

    quantities = []
    for d in range(B):
        tile = values_of(d)
        edge = [jnp.broadcast_to(got[d * R + 8 + q : d * R + 9 + q, :], (8, L)) for q in range(5)]
        quantities.append(
            [jnp.where(lane >= LEFT, edge[q], rolled(tile, -PER * q)) for q in range(5)]
        )
    off = [quantities[d][1] for d in range(B)]

    def joined(here, above, sign):
        return [
            here[d] + sign * above[d + 1] if d < B - 1 else here[d] for d in range(B)
        ]

    diag = joined([v[2] for v in quantities], [v[0] for v in quantities], -1.0)
    right = joined([v[4] for v in quantities], [v[3] for v in quantities], 1.0)
    middle = B // 2
    up, down = {}, {}
    for n in range(middle):
        d = n
        pivot = diag[d] - off[d] * up[d - 1][1] if n else diag[d]
        inverse = 1.0 / pivot
        up[d] = (inverse, off[d + 1] * inverse)
        d = B - 1 - n
        if d > middle:
            pivot = diag[d] - off[d + 1] * down[d + 1][1] if n else diag[d]
            inverse = 1.0 / pivot
            down[d] = (inverse, off[d] * inverse)
    centre = diag[middle] - off[middle] * up[middle - 1][1] - off[middle + 1] * down[middle + 1][1]
    centre = 1.0 / centre

    def solved(right):
        ahead, behind, values = {}, {}, [None] * B
        for n in range(middle):
            d = n
            total = right[d] + off[d] * ahead[d - 1] if n else right[d]
            ahead[d] = total * up[d][0]
            d = B - 1 - n
            if d > middle:
                total = right[d] + off[d + 1] * behind[d + 1] if n else right[d]
                behind[d] = total * down[d][0]
        total = right[middle] + off[middle] * ahead[middle - 1] + off[middle + 1] * behind[middle + 1]
        values[middle] = total * centre
        for n in range(middle):
            d = middle - 1 - n
            values[d] = ahead[d] + up[d][1] * values[d + 1]
            d = middle + 1 + n
            if d < B:
                values[d] = behind[d] + down[d][1] * values[d - 1]
        return values

    around = []
    for value in solved(right):
        first = jnp.where(tint == 1.0, 0.0, value)
        around.append(
            (
                rolled(first, 1),
                rolled(first, -1),
                jnp.where(line == 0, rolled(value, 1 - LEFT), pltpu.roll(first, 1, 0)),
                jnp.where(line == 7, rolled(value, 1 - RIGHT), pltpu.roll(first, 7, 0)),
            )
        )
    still = jnp.zeros((8, L), jnp.float32)
    added = []
    for d in range(B):
        tile, extra = couplings(d), values_of(d)
        totals = []
        for a in range(2):
            total = still
            for b in range(2):
                i, j = 2 * a + b, 2 * b + a
                here = around[d - 1 + b] if d - 1 + b >= 0 else None
                if here is None:
                    continue
                total = total + rolled(tile, 1 - 64 - 16 * i) * here[0]
                after = jnp.where(
                    lane == X, rolled(extra, X - HIGH_LINK - i), rolled(tile, -64 - 16 * j)
                )
                total = total + after * here[1]
                link = got[d * R + 8 + (5 + i if i < 3 else 5) :, :][:1]
                link = rolled(link, 1 - LEFT if i < 3 else 1 - RIGHT)
                back = jnp.where(line == 0, link, pltpu.roll(rolled(tile, 1 - 16 * j), 1, 0))
                total = total + back * here[2]
                total = total + rolled(tile, 1 - 16 * i) * here[3]
            totals.append(jnp.where(tint == 1.0, total, 0.0))
        added.append(totals)
    second = joined(
        [quantities[d][4] + added[d][1] for d in range(B)],
        [quantities[d][3] + added[d][0] for d in range(B)],
        1.0,
    )
    before = still
    ends[0:8, :] = still
    for d, value in enumerate(solved(second)):
        pair = jnp.where(lane < 32, value, pltpu.roll(pltpu.roll(value, 32, 1), 4, 0))
        both = jnp.where(lane < 64, pair, pltpu.roll(before, 64, 1))
        out[4 * d : 4 * d + 4, :] = both[:4]
        ends[8 + d : 9 + d, :] = value[0:1]
        before = pair

    shift = jnp.where(patch == 0, PER - LEFT + L, PER - RIGHT + L)
    here, below = ends[8 : 8 + B, :], ends[7 : 7 + B, :]
    lanes = iota((B, L), 1)
    for i in range(2):
        rows = out[pl.ds(i, B, stride=4), :]
        rows = jnp.where(
            (lanes >= PER) & (lanes < PER + 8), pltpu.roll(here, shift - 8 * i, 1), rows
        )
        rows = jnp.where(
            (lanes >= PER + 64) & (lanes < PER + 72), pltpu.roll(below, shift + 64 - 8 * i, 1), rows
        )
        out[pl.ds(i, B, stride=4), :] = rows


def finish_kernel(
    coef, source, inv, h_source, h_inv, colour, known, e_first, e_last, got, out, v_first, h_line
):
    spacing, face = coefficient_rows(coef, Y)
    h_face = coefficient_rows(coef, L)[1]
    left_core = lax.axis_index("gy") == 0
    mine = colour[...]

    upper = iota((8, L), 0) < 4
    tiles = []
    for n in range(B // 2):
        near = got[8 * n : 8 * n + 8, :]
        far = pltpu.roll(near, L - 32, 1)
        tiles.append(jnp.where(upper, near, pltpu.roll(far, 4, 0)))
        tiles.append(jnp.where(upper, pltpu.roll(near, 4, 0), far))
    halves = [jnp.concatenate(tiles[c * L // 8 : (c + 1) * L // 8], 0) for c in range(2)]
    turned = jnp.concatenate([jnp.transpose(half) for half in halves], 1)
    low, high = turned[65 : 65 + X], turned[1 : 1 + X]
    nothing = jnp.zeros((1, L), jnp.float32)
    outer = jnp.where(left_core, tiles[-1], tiles[0])

    def beside(b):
        at_b = 0 if b else 64
        moved = pltpu.roll(outer, L - PER - at_b, 1)
        end = jnp.where(iota((1, L), 1) < 8, moved[0:1], pltpu.roll(moved[1:2], 8, 1))
        lo, hi = turned[at_b : at_b + 1], turned[at_b + 1 + X : at_b + 2 + X]
        places = {XHI: hi[:, :L], XHI + 1: hi[:, L:], XLO0: lo[:, :L], XLO1: lo[:, L:], YH: end}
        return jnp.concatenate([places.get(p, nothing) for p in range(8)], 0)

    beside_after_first(h_face, h_source, h_inv, beside(0), beside(1), h_line)
    columns = sided(transposed(h_line[pl.ds(YH, D, stride=8), :]))
    low_first, high_first = jnp.where(mine == 0, low, 0.0), jnp.where(mine == 0, high, 0.0)
    for k in range(D):
        value = known[at(k), :] + e_first[at(k), :] * low_first
        v_first[at(k), :] = value + e_last[at(k), :] * high_first
    value = low
    for k in range(D - 1):
        added = beside_sum(v_first, h_line, columns, k)
        value = (source[at(k), :] + spacing[k] * added + face[k] * value) * inv[at(k), :]
        out[at(k), :] = value
    value = high
    for k in range(D - 1, -1, -1):
        if k < D - 1:
            value = out[at(k), :] + (face[k + 1] * inv[at(k), :]) * value
        out[at(k), :] = jnp.where(mine == 0, v_first[at(k), :], value)


VMEM = pl.BlockSpec(memory_space=pltpu.VMEM)
ANY = pl.BlockSpec(memory_space=pl.ANY)
SMEM = pl.BlockSpec(memory_space=pltpu.SMEM)


def f32(*shape):
    return jax.ShapeDtypeStruct(shape, jnp.float32)


def call(kernel, outs, specs, scratch, cost, *args, vmem=32):
    return pl.pallas_call(
        kernel,
        out_shape=outs,
        in_specs=specs,
        out_specs=jax.tree.map(lambda _: VMEM, outs),
        scratch_shapes=[
            pltpu.VMEM(s, jnp.float32) if isinstance(s, tuple) else s for s in scratch
        ],
        compiler_params=pltpu.CompilerParams(vmem_limit_bytes=vmem * 1024 * 1024),
        cost_estimate=pl.CostEstimate(flops=cost, bytes_accessed=cost, transcendentals=0),
    )(*args)


def on_device(correction, residual, state, level, colour):
    corr, res, st = (v.reshape(D * X, Y) for v in (correction, residual, state))
    own_lo, own_hi = call(
        pack_x_kernel, (f32(72, Y), f32(72, Y)), [ANY] * 4,
        [pltpu.VMEM((X, Y), jnp.int32), pltpu.SemaphoreType.DMA((9,))],
        1 << 20, correction, residual, state, colour, vmem=60,
    )
    xs = lax.axis_size("gx")
    ring = [(i, (i + 1) % xs) for i in range(xs)]
    got_lo = lax.ppermute(own_hi, "gx", ring)
    got_hi = lax.ppermute(own_lo, "gx", [(b, a) for a, b in ring])
    own_y, tints = call(
        pack_y_kernel, (f32(8, Y), f32(Y, L)), [VMEM] * 4, [], 1 << 20, corr, res, st, colour
    )
    swap = [(0, 1), (1, 0)]
    got_y = lax.ppermute(own_y, "gy", swap)
    field = f32(D * X, Y)
    inv, e_first, e_last, k_own, w_x, w_y, coef = call(
        factor_kernel,
        (field, field, field, f32(3 * X, Y), f32(4 * X, Y), f32(4 * X, Y), f32(40, Y)),
        [SMEM, VMEM], [], 1 << 22, level, st,
    )
    got_lo, got_hi, got_y, inv = lax.optimization_barrier((got_lo, got_hi, got_y, inv))
    cross_lo = lax.ppermute(got_lo[:D], "gy", swap)
    cross_hi = lax.ppermute(got_hi[:D], "gy", swap)
    small = f32(8 * D, L)
    source, v_first, h_local, h_inv, h_first, h_last, h_mask, coupled, laid = call(
        local_kernel, (field, field, small, small, small, small, f32(8, L), f32(Y, L), f32(L, Y)),
        [VMEM] * 16, [(8 * D, L), (8 * D, L), (L, Y)], 1 << 22,
        coef, corr, res, colour, inv, e_first, e_last, k_own, w_x, w_y,
        own_lo, own_hi, got_lo, got_hi, own_y, got_y,
    )
    message, h_source = call(
        message_kernel, (f32(B * R, L), small), [VMEM] * 15, [(8 * D, L), (L, Y)], 1 << 22,
        coef, colour, source, v_first, h_local, h_inv, h_first, h_last, h_mask, coupled, laid,
        e_first, e_last, cross_lo, cross_hi,
    )

    def exchanged(value, rows):
        blocks = value.reshape(B, rows, L)
        return lax.all_to_all(blocks, "gz", 0, 0, tiled=True).reshape(B * rows, L)

    separators = call(
        separator_kernel, f32(B * 4, L), [VMEM] * 2, [(B + 8, L)],
        1 << 21, exchanged(message, R), tints,
    )
    out = call(
        finish_kernel, field, [VMEM] * 10, [(D * X, Y), (8 * D, L)], 1 << 21,
        coef, source, inv, h_source, h_inv, colour, v_first, e_first, e_last,
        exchanged(separators, 4),
    )
    return out.reshape(D, X, Y)


def solution(mesh):
    block = P("gz", "gx", "gy")
    return jax.shard_map(
        on_device,
        mesh=mesh,
        in_specs=(block, block, block, P(), P("gx", "gy")),
        out_specs=block,
        check_vma=False,
    )
```

```python
import jax
import jax.numpy as jnp
from jax import lax
from jax.experimental import pallas as pl
from jax.experimental.pallas import tpu as pltpu
from jax.sharding import PartitionSpec as P

coef_z = 1000.0
coef_x = 0.3
coef_y = 0.2
bratu_lambda = 0.2

D = 16
X = 16
Y = 256
L = 128
B = 32
R = 16

XHI, YH, XLO0, OWN15, YOWN, XLO1 = 0, 2, 3, 4, 6, 7
PER, HIGH_LINK, LEFT, RIGHT = 18, 90, 96, 112
TURNED = (0, 2, 1, 3)


def iota(shape, dim):
    return lax.broadcasted_iota(jnp.int32, shape, dim)


def row_coefficients(level_ref):
    base = lax.axis_index("gz") * D
    last = level_ref.shape[0] - 1

    def spacing(row):
        level = level_ref[jnp.clip(base + row, 0, last)]
        once = jnp.where((level & 1) == 1, jnp.float32(1.3), jnp.float32(1.0))
        twice = jnp.where((level & 2) == 2, jnp.float32(1.3 * 1.3), jnp.float32(1.0))
        return jnp.float32(0.8) * (once * twice)

    around = [spacing(row) for row in range(-1, D + 1)]
    faces = []
    for i in range(D + 1):
        inside = (base + i > 0) & (base + i <= last)
        face = jnp.float32(coef_z * 2.0) / (around[i] + around[i + 1])
        faces.append(jnp.where(inside, face, jnp.float32(0.0)))
    return around[1 : D + 1], faces


def coefficient_rows(coef, width):
    return (
        [coef[k : k + 1, :width] for k in range(D)],
        [coef[D + k : D + k + 1, :width] for k in range(D + 1)],
    )


def centre_of(spacing, low, high, state):
    return (low + high) + spacing * ((2.0 * coef_x + 2.0 * coef_y) - bratu_lambda * jnp.exp(state))


def transposed(rows):
    short = L - rows.shape[0]
    if short:
        rows = jnp.concatenate([rows, jnp.zeros((short, L), rows.dtype)], 0)
    return jnp.transpose(rows)


def at(k):
    return slice(k * X, (k + 1) * X)


def beside_after_first(face, h_source, h_inv, low, high, h_line):
    value = low
    forwards = []
    for k in range(D - 1):
        rows = slice(k * 8, (k + 1) * 8)
        value = (h_source[rows, :] + face[k] * value) * h_inv[rows, :]
        forwards.append(value)
    value = high
    h_line[(D - 1) * 8 :, :] = value
    for k in range(D - 2, -1, -1):
        rows = slice(k * 8, (k + 1) * 8)
        value = forwards[k] + (face[k + 1] * h_inv[rows, :]) * value
        h_line[rows, :] = value


def own_after_first(face, source, inv, tint, low, high, v_first):
    value = low
    for k in range(D - 1):
        value = (source[at(k), :] + face[k] * value) * inv[at(k), :]
        v_first[at(k), :] = value
    value = high
    for k in range(D - 1, -1, -1):
        if k < D - 1:
            value = v_first[at(k), :] + (face[k + 1] * inv[at(k), :]) * value
        v_first[at(k), :] = jnp.where(tint == 0, value, 0.0)


def sided(columns):
    left = jnp.full(columns.shape, lax.axis_index("gy"), jnp.int32) == 0
    return jnp.where(left, 0.0, columns), jnp.where(left, columns, 0.0)


def beside_sum(v_first, h_line, columns, k):
    row, lane = iota((X, Y), 0), iota((X, Y), 1)
    lines = v_first[at(k), :]
    sides = h_line[k * 8 : (k + 1) * 8, :]
    lo = jnp.concatenate([sides[XLO0 : XLO0 + 1], sides[XLO1 : XLO1 + 1]], 1)
    hi = jnp.concatenate([sides[XHI : XHI + 1], sides[XHI + 1 : XHI + 2]], 1)

    left_column, right_column = (c[:X, k : k + 1] for c in columns)
    left = jnp.where(lane == 0, left_column, pltpu.roll(lines, 1, 1))
    right = jnp.where(lane == Y - 1, right_column, pltpu.roll(lines, Y - 1, 1))
    in_x = jnp.where(row == 0, lo, pltpu.roll(lines, 1, 0)) + jnp.where(
        row == X - 1, hi, pltpu.roll(lines, X - 1, 0)
    )
    return coef_x * in_x + coef_y * (left + right)


def pack_x_kernel(corr, res, state, colour, lo, hi, tint, arrived):
    copies = []
    for out, edge, inner in ((lo, 0, 1), (hi, X - 1, X - 2)):
        for i, (ref, x) in enumerate(((corr, edge), (corr, inner), (res, edge), (state, edge))):
            rows = out.at[pl.ds(i * D, D), :]
            copies.append(pltpu.make_async_copy(ref.at[:, x, :], rows, arrived.at[len(copies)]))
    copies.append(pltpu.make_async_copy(colour, tint, arrived.at[len(copies)]))
    for copy in copies:
        copy.start()
    for copy in copies:
        copy.wait()
    for out, edge in ((lo, 0), (hi, X - 1)):
        row = tint[edge : edge + 1, :].astype(jnp.float32)
        out[4 * D : 4 * D + 8, :] = jnp.broadcast_to(row, (8, Y))


def pack_y_kernel(corr, res, state, colour, out, tint):
    left_core = lax.axis_index("gy") == 0

    def columns(value):
        near = jnp.where(left_core, value[:, L:], value[:, :L])
        return jnp.concatenate([transposed(near[i : i + L]) for i in range(0, near.shape[0], L)], 1)

    def picked(turned, inner):
        return jnp.where(left_core, turned[L - 1 - inner : L - inner], turned[inner : inner + 1])

    field = columns(corr[...])
    out[0:1, :] = picked(field, 0)
    out[1:2, :] = picked(field, 1)
    out[2:3, :] = picked(columns(res[...]), 0)
    out[3:4, :] = picked(columns(state[...]), 0)
    row = picked(columns(colour[...].astype(jnp.float32)), 0)
    out[4:8, :] = jnp.broadcast_to(jnp.concatenate([row, row], 1), (4, Y))
    shifted = jnp.concatenate([jnp.zeros((1, Y), jnp.float32), colour[...].astype(jnp.float32)], 0)
    for c in range(2):
        tint[c * L : (c + 1) * L, :] = transposed(shifted[:, c * L : (c + 1) * L])


def factor_kernel(level, state, inv, e_first, e_last, k_own, w_x, w_y, coef):
    spacing, face = row_coefficients(level)
    for i, value in enumerate(spacing + face):
        coef[i : i + 1, :] = jnp.full((1, Y), value, jnp.float32)
    for i in range(2 * D + 1, coef.shape[0]):
        coef[i : i + 1, :] = jnp.zeros((1, Y), jnp.float32)

    def rows(ref, k):
        return ref[k * X : (k + 1) * X, :]

    ratios, forward = [], []
    ratio = running = None
    for k in range(D - 1):
        pivot = centre_of(spacing[k], face[k], face[k + 1], rows(state, k))
        if k:
            pivot = pivot - face[k] * ratio
        inverse = 1.0 / pivot
        scaled = face[k] * inverse
        running = scaled * running if k else scaled
        ratio = face[k + 1] * inverse
        inv[k * X : (k + 1) * X, :] = inverse
        e_first[k * X : (k + 1) * X, :] = running
    inv[(D - 1) * X :, :] = jnp.zeros((X, Y), jnp.float32)
    e_first[(D - 1) * X :, :] = jnp.zeros((X, Y), jnp.float32)
    e_last[(D - 1) * X :, :] = jnp.ones((X, Y), jnp.float32)
    zero, one = jnp.zeros((X, Y), jnp.float32), jnp.ones((X, Y), jnp.float32)
    first, last = zero, one
    wx = [zero, zero, zero, one * (coef_x * spacing[D - 1])]
    wy = [zero, zero, zero, one * (coef_y * spacing[D - 1])]
    for k in range(D - 2, -1, -1):
        ratio = face[k + 1] * rows(inv, k)
        first = rows(e_first, k) + ratio * first
        last = ratio * last
        e_first[k * X : (k + 1) * X, :] = first
        e_last[k * X : (k + 1) * X, :] = last
        if k == D - 2:
            k_own[X : 2 * X, :] = face[D - 1] * first
            centre = centre_of(spacing[D - 1], face[D - 1], face[D], rows(state, D - 1))
            k_own[2 * X :, :] = centre - face[D - 1] * last
        before = (pltpu.roll(first, 1, 0), pltpu.roll(last, 1, 0))
        after = (pltpu.roll(first, Y - 1, 1), pltpu.roll(last, Y - 1, 1))
        for a, mine in enumerate((first, last)):
            in_x, in_y = (coef_x * spacing[k]) * mine, (coef_y * spacing[k]) * mine
            for b in range(2):
                wx[2 * a + b] = wx[2 * a + b] + in_x * before[b]
                wy[2 * a + b] = wy[2 * a + b] + in_y * after[b]
    k_own[:X, :] = face[0] * first
    for i in range(4):
        w_x[i * X : (i + 1) * X, :] = wx[i]
        w_y[i * X : (i + 1) * X, :] = wy[i]


def local_kernel(
    coef, corr, res, colour, inv, e_first, e_last, k_own, w_x, w_y,
    own_lo, own_hi, got_lo, got_hi, own_y, got_y,
    source, v_first, h_source, h_inv, h_first, h_last, h_mask, coupled, laid,
    y_scratch, h_state, pairs,
):
    spacing, face = coefficient_rows(coef, Y)
    h_spacing, h_face = coefficient_rows(coef, L)
    has_lo, has_hi = lax.axis_index("gx") > 0, lax.axis_index("gx") < lax.axis_size("gx") - 1
    row = iota((X, Y), 0)
    lane = iota((X, Y), 1)

    def plane(ref, i):
        return ref[i * D : (i + 1) * D, :]

    def spread(ref):
        for k in range(D):
            first = k % 8 * X
            tile = ref[:, k // 8 * L : (k // 8 + 1) * L]
            y_scratch[k * 8 : (k + 1) * 8, :] = pltpu.roll(tile, L - first, 1) if first else tile
        return [y_scratch[pl.ds(q, D, stride=8), :] for q in range(5)]

    yh_corr, yh_next, yh_res, yh_state, yh_colour = spread(got_y)
    yo_corr, unused, unused, yo_state, unused = spread(own_y)
    yh_colour = yh_colour[0:1]

    h_state[...] = jnp.zeros_like(h_state)
    h_source[...] = jnp.zeros_like(h_source)
    h_mask[...] = jnp.zeros_like(h_mask)

    small_lane = iota((D, L), 1)
    below = jnp.where(small_lane == 0, 0.0, pltpu.roll(yh_corr, 1, 1))
    above = jnp.where(small_lane == X - 1, 0.0, pltpu.roll(yh_corr, L - 1, 1))
    yh_source = yh_res + (coef_x * (below + above) + coef_y * (yo_corr + yh_next))
    h_source[pl.ds(YH, D, stride=8), :] = jnp.where(yh_colour == 0.0, yh_source, 0.0)
    h_mask[YH : YH + 1, :] = jnp.where(yh_colour == 0.0, 1.0, 0.0)
    h_state[pl.ds(YH, D, stride=8), :] = yh_state
    h_state[pl.ds(YOWN, D, stride=8), :] = yo_state
    beside_corr = []
    lane_k = iota((D, Y), 1)
    for got, own, there, places in (
        (got_lo, own_lo, has_lo, (XLO0, XLO1)),
        (got_hi, own_hi, has_hi, (XHI, XHI + 1)),
    ):
        near = jnp.where(there, plane(got, 0), 0.0)
        beside_corr.append(near)
        left = jnp.where(lane_k == 0, 0.0, pltpu.roll(near, 1, 1))
        right = jnp.where(lane_k == Y - 1, 0.0, pltpu.roll(near, Y - 1, 1))
        value = plane(got, 2) + (coef_x * (plane(got, 1) + plane(own, 0)) + coef_y * (left + right))
        mask = jnp.where(there & (got[4 * D : 4 * D + 1, :] == 0.0), 1.0, 0.0)
        value = jnp.where(mask == 1.0, value, 0.0)
        states = plane(got, 3)
        for c, place in enumerate(places):
            h_source[pl.ds(place, D, stride=8), :] = value[:, c * L : (c + 1) * L]
            h_mask[place : place + 1, :] = mask[:, c * L : (c + 1) * L]
            h_state[pl.ds(place, D, stride=8), :] = states[:, c * L : (c + 1) * L]
    edge_state = plane(own_hi, 3)
    for c in range(2):
        h_state[pl.ds(OWN15 + c, D, stride=8), :] = edge_state[:, c * L : (c + 1) * L]

    def rows8(ref, k):
        return ref[k * 8 : (k + 1) * 8, :]

    ratio = running = None
    inverses, forwards = [], []
    for k in range(D - 1):
        pivot = centre_of(h_spacing[k], h_face[k], h_face[k + 1], rows8(h_state, k))
        if k:
            pivot = pivot - h_face[k] * ratio
        inverse = 1.0 / pivot
        scaled = h_face[k] * inverse
        running = scaled * running if k else scaled
        ratio = h_face[k + 1] * inverse
        inverses.append(inverse)
        forwards.append(running)
        h_inv[k * 8 : (k + 1) * 8, :] = inverse
    h_inv[(D - 1) * 8 :, :] = jnp.zeros((8, L), jnp.float32)
    zero, one = jnp.zeros((8, L), jnp.float32), jnp.ones((8, L), jnp.float32)
    place8 = iota((8, L), 0)
    weight = jnp.where((place8 == YOWN) | (place8 == YH), jnp.float32(coef_y), jnp.float32(coef_x))
    first, last = zero, one
    hw = [zero, zero, zero, weight * h_spacing[D - 1]]
    h_source[(D - 1) * 8 :, :] = h_spacing[D - 1] * rows8(h_source, D - 1)
    hk = [None, None, None]
    h_first[(D - 1) * 8 :, :] = zero
    h_last[(D - 1) * 8 :, :] = one
    for k in range(D - 2, -1, -1):
        ratio = h_face[k + 1] * inverses[k]
        first = forwards[k] + ratio * first
        last = ratio * last
        if k == D - 2:
            hk[1] = h_face[D - 1] * first
            centre = centre_of(h_spacing[D - 1], h_face[D - 1], h_face[D], rows8(h_state, D - 1))
            hk[2] = centre - h_face[D - 1] * last
        h_source[k * 8 : (k + 1) * 8, :] = h_spacing[k] * rows8(h_source, k)
        h_first[k * 8 : (k + 1) * 8, :] = first
        h_last[k * 8 : (k + 1) * 8, :] = last
        partner = (pltpu.roll(first, 4, 0), pltpu.roll(last, 4, 0))
        for a, mine in enumerate((first, last)):
            mine = (weight * h_spacing[k]) * mine
            for b in range(2):
                hw[2 * a + b] = hw[2 * a + b] + mine * partner[b]
    hk[0] = h_face[0] * first

    columns = transposed(
        jnp.concatenate([v[YH : YH + 1] for v in hk] + [v[YOWN : YOWN + 1] for v in hw], 0)
    )
    columns_corr = sided(transposed(jnp.concatenate([yh_corr, yh_colour], 0)))

    mine = colour[...]
    colour_lo, colour_hi = got_lo[4 * D : 4 * D + 1, :], got_hi[4 * D : 4 * D + 1, :]
    tint = mine.astype(jnp.float32)
    at_left, at_right = (lane == 0), (lane == Y - 1)

    def beside_of(value, lo, hi, k):
        return (
            jnp.where(row == 0, lo, pltpu.roll(value, 1, 0)),
            jnp.where(row == X - 1, hi, pltpu.roll(value, X - 1, 0)),
            jnp.where(at_left, columns_corr[0][:X, k : k + 1], pltpu.roll(value, 1, 1)),
            jnp.where(at_right, columns_corr[1][:X, k : k + 1], pltpu.roll(value, Y - 1, 1)),
        )

    weights = [
        jnp.where((tint == 1.0) & (other == 0.0), 0.0, jnp.float32(amount))
        for other, amount in zip(
            beside_of(tint, colour_lo, colour_hi, D), (coef_x, coef_x, coef_y, coef_y)
        )
    ]
    for k in range(D):
        around = beside_of(
            corr[at(k), :], beside_corr[0][k : k + 1], beside_corr[1][k : k + 1], k
        )
        total = res[at(k), :]
        for w, v in zip(weights, around):
            total = total + w * v
        source[at(k), :] = spacing[k] * total
    still = jnp.zeros((X, Y), jnp.float32)
    own_after_first(face, source, inv, mine, still, still, v_first)

    masks = end_masks()
    slot = lane & 7
    left_slots = right_slots = still
    for q in range(3):
        own = k_own[q * X : (q + 1) * X, :]
        put_lines(laid, q, hk[q], own)
        left, right = end_slots(masks, q, columns[:X, q : q + 1], own, own)
        left_slots = jnp.where(slot == q, left, left_slots)
        right_slots = jnp.where(slot == q, right, right_slots)
    for i, j in enumerate(TURNED):
        link = columns[:X, 3 + i : 4 + i]
        along = w_y[i * X : (i + 1) * X, :]
        pairs[i * X : (i + 1) * X, :] = jnp.where(masks[2], link, along)
        along = jnp.where(masks[1], link, w_y[j * X : (j + 1) * X, :])
        if i < 3:
            left_slots = jnp.where(slot == 5 + i, pltpu.roll(along, 6 + i, 1), left_slots)
        else:
            right_slots = jnp.where(slot == 5, pltpu.roll(along, 6, 1), right_slots)
        high = jnp.concatenate([hw[i][OWN15 : OWN15 + 1], hw[i][OWN15 + 1 : OWN15 + 2]], 1)
        laid[HIGH_LINK + i : HIGH_LINK + i + 1, :] = high
    laid[PER * 3 : PER * 5, :] = jnp.zeros((PER * 2, Y), jnp.float32)
    laid[HIGH_LINK + 4 : LEFT, :] = jnp.zeros((LEFT - HIGH_LINK - 4, Y), jnp.float32)
    laid[LEFT:RIGHT, :] = left_slots
    laid[RIGHT:, :] = right_slots

    amounts = coef_x * coef[0:D, 0:1]
    edges = [
        amounts * jnp.concatenate([e[k * X : k * X + 1, :] for k in range(D)], 0)
        for e in (e_first, e_last)
    ]
    lows = [
        jnp.concatenate([h[pl.ds(p, D, stride=8), :] for p in (XLO0, XLO1)], 1)
        for h in (h_first, h_last)
    ]
    for a in range(2):
        for b in range(2):
            i = 2 * a + b
            edge = jnp.sum(edges[a] * lows[b], axis=0, keepdims=True)
            along = w_x[i * X : (i + 1) * X, :]
            pairs[(4 + i) * X : (5 + i) * X, :] = jnp.where(row == 0, edge, along)
    for c in range(2):
        coupled[c * L : (c + 1) * L, :] = jnp.transpose(pairs[:, c * L : (c + 1) * L])


def end_masks():
    lane = iota((X, Y), 1)
    is_left = jnp.full((X, Y), lax.axis_index("gy"), jnp.int32) == 0
    at_left, at_right = (lane == 0), (lane == Y - 1)
    return at_left & is_left, at_right & ~is_left, at_right & is_left, at_left & ~is_left


def end_slots(masks, q, outer, seen, nothing):
    outer_left, outer_right, none_left, none_right = masks
    before = jnp.where(outer_right, outer, jnp.where(none_left, nothing, seen))
    behind = jnp.where(outer_left, outer, jnp.where(none_right, nothing, seen))
    return pltpu.roll(before, 1 + q, 1), pltpu.roll(behind, Y - 8 + q, 1)


def put_lines(laid, q, side, own):
    low = jnp.concatenate([side[XLO0 : XLO0 + 1], side[XLO1 : XLO1 + 1]], 1)
    high = jnp.concatenate([side[XHI : XHI + 1], side[XHI + 1 : XHI + 2]], 1)
    laid[PER * q : PER * q + 1, :] = low
    laid[PER * q + 1 : PER * q + 1 + X, :] = own
    laid[PER * q + 1 + X : PER * q + 2 + X, :] = high


def message_kernel(
    coef, colour, source, v_first, h_local, h_inv, h_first, h_last, h_mask, coupled, local,
    e_first, e_last, crossed,
    message, h_source, h_line, laid,
):
    spacing, face = coefficient_rows(coef, Y)
    h_face = coefficient_rows(coef, L)[1]
    on_left = jnp.where(lax.axis_index("gy") == 0, jnp.float32(1.0), jnp.float32(0.0))
    lane = iota((X, Y), 1)
    small_lane = iota((D, L), 1)
    amounts = coef[0:D, 0:1]
    h_source[...] = h_local[...]
    laid[...] = local[...]

    def add(place, lane_at, value):
        rows = h_source[pl.ds(place, D, stride=8), :]
        rows = rows + jnp.where(small_lane == lane_at, value, 0.0) * h_mask[place : place + 1, :]
        h_source[pl.ds(place, D, stride=8), :] = rows

    xs = lax.axis_size("gx") - 1
    cross_lo, cross_hi = crossed[0:D, :], crossed[D:, :]
    for cross, there, places, lane_at in (
        (cross_lo, lax.axis_index("gx") > 0, (XLO0, XLO1), 0),
        (cross_hi, lax.axis_index("gx") < xs, (XHI, XHI + 1), X - 1),
    ):
        value = on_left * cross[:, 0:1] + (1.0 - on_left) * cross[:, Y - 1 : Y]
        value = amounts * jnp.where(there, value, 0.0)
        add(YH, lane_at, coef_x * value)
        add(places[0], 0, (coef_y * (1.0 - on_left)) * value)
        add(places[1], L - 1, (coef_y * on_left) * value)

    zero = jnp.zeros((8, L), jnp.float32)
    hf = [zero, zero]
    for k in range(D):
        rows = slice(k * 8, (k + 1) * 8)
        hf[0] = hf[0] + h_first[rows, :] * h_source[rows, :]
        hf[1] = hf[1] + h_last[rows, :] * h_source[rows, :]
    columns = transposed(jnp.concatenate([v[YH : YH + 1] for v in hf], 0))

    beside_after_first(h_face, h_source, h_inv, zero, zero, h_line)
    columns_first = sided(transposed(h_line[pl.ds(YH, D, stride=8), :]))
    mine = colour[...]
    still = jnp.zeros((X, Y), jnp.float32)
    f_own = [still, still]
    for k in range(D):
        added = beside_sum(v_first, h_line, columns_first, k)
        total = source[at(k), :] + jnp.where(mine == 1, spacing[k] * added, 0.0)
        f_own[0] = f_own[0] + e_first[at(k), :] * total
        f_own[1] = f_own[1] + e_last[at(k), :] * total

    masks = end_masks()
    slot = lane & 7
    left_slots, right_slots = laid[LEFT:RIGHT, :], laid[RIGHT:, :]
    for i in range(2):
        q = 3 + i
        put_lines(laid, q, hf[i], f_own[i])
        seen = jnp.where(mine == 0, f_own[i], 0.0)
        left, right = end_slots(masks, q, columns[:X, i : i + 1], seen, still)
        left_slots = jnp.where(slot == q, left, left_slots)
        right_slots = jnp.where(slot == q, right, right_slots)
    laid[LEFT:RIGHT, :] = left_slots
    laid[RIGHT:, :] = right_slots
    for c in range(2):
        turned = jnp.transpose(laid[:, c * L : (c + 1) * L])
        for n in range(L // 8):
            p = c * (L // 8) + n
            message[p * R : p * R + 8, :] = coupled[8 * p : 8 * p + 8, :]
            message[p * R + 8 : p * R + 16, :] = turned[8 * n : 8 * n + 8]


def separator_kernel(got, tints, out, ends):
    patch = lax.axis_index("gz")
    tint = tints[pl.ds(pl.multiple_of(patch * 8, 8), 8), :]
    line, lane = iota((8, L), 0), iota((8, L), 1)

    def rolled(value, amount):
        amount = amount % L
        return pltpu.roll(value, amount, 1) if amount else value

    def couplings(d):
        return got[d * R : d * R + 8, :]

    def values_of(d):
        return got[d * R + 8 : d * R + 16, :]

    quantities = []
    for d in range(B):
        tile = values_of(d)
        edge = [jnp.broadcast_to(got[d * R + 8 + q : d * R + 9 + q, :], (8, L)) for q in range(5)]
        quantities.append(
            [jnp.where(lane >= LEFT, edge[q], rolled(tile, -PER * q)) for q in range(5)]
        )
    off = [quantities[d][1] for d in range(B)]

    def joined(here, above, sign):
        return [
            here[d] + sign * above[d + 1] if d < B - 1 else here[d] for d in range(B)
        ]

    diag = joined([v[2] for v in quantities], [v[0] for v in quantities], -1.0)
    right = joined([v[4] for v in quantities], [v[3] for v in quantities], 1.0)
    middle = B // 2
    up, down = {}, {}
    for n in range(middle):
        d = n
        pivot = diag[d] - off[d] * up[d - 1][1] if n else diag[d]
        inverse = 1.0 / pivot
        up[d] = (inverse, off[d + 1] * inverse)
        d = B - 1 - n
        if d > middle:
            pivot = diag[d] - off[d + 1] * down[d + 1][1] if n else diag[d]
            inverse = 1.0 / pivot
            down[d] = (inverse, off[d] * inverse)
    centre = diag[middle] - off[middle] * up[middle - 1][1] - off[middle + 1] * down[middle + 1][1]
    centre = 1.0 / centre

    def solved(right):
        ahead, behind, values = {}, {}, [None] * B
        for n in range(middle):
            d = n
            total = right[d] + off[d] * ahead[d - 1] if n else right[d]
            ahead[d] = total * up[d][0]
            d = B - 1 - n
            if d > middle:
                total = right[d] + off[d + 1] * behind[d + 1] if n else right[d]
                behind[d] = total * down[d][0]
        total = right[middle] + off[middle] * ahead[middle - 1] + off[middle + 1] * behind[middle + 1]
        values[middle] = total * centre
        for n in range(middle):
            d = middle - 1 - n
            values[d] = ahead[d] + up[d][1] * values[d + 1]
            d = middle + 1 + n
            if d < B:
                values[d] = behind[d] + down[d][1] * values[d - 1]
        return values

    around = []
    for value in solved(right):
        first = jnp.where(tint == 1.0, 0.0, value)
        around.append(
            (
                rolled(first, 1),
                rolled(first, -1),
                jnp.where(line == 0, rolled(value, 1 - LEFT), pltpu.roll(first, 1, 0)),
                jnp.where(line == 7, rolled(value, 1 - RIGHT), pltpu.roll(first, 7, 0)),
            )
        )
    still = jnp.zeros((8, L), jnp.float32)
    added = []
    for d in range(B):
        tile, extra = couplings(d), values_of(d)
        totals = []
        for a in range(2):
            total = still
            for b in range(2):
                i, j = 2 * a + b, 2 * b + a
                here = around[d - 1 + b] if d - 1 + b >= 0 else None
                if here is None:
                    continue
                total = total + rolled(tile, 1 - 64 - 16 * i) * here[0]
                after = jnp.where(
                    lane == X, rolled(extra, X - HIGH_LINK - i), rolled(tile, -64 - 16 * j)
                )
                total = total + after * here[1]
                link = got[d * R + 8 + (5 + i if i < 3 else 5) :, :][:1]
                link = rolled(link, 1 - LEFT if i < 3 else 1 - RIGHT)
                back = jnp.where(line == 0, link, pltpu.roll(rolled(tile, 1 - 16 * j), 1, 0))
                total = total + back * here[2]
                total = total + rolled(tile, 1 - 16 * i) * here[3]
            totals.append(jnp.where(tint == 1.0, total, 0.0))
        added.append(totals)
    second = joined(
        [quantities[d][4] + added[d][1] for d in range(B)],
        [quantities[d][3] + added[d][0] for d in range(B)],
        1.0,
    )
    before = still
    ends[0:8, :] = still
    for d, value in enumerate(solved(second)):
        pair = jnp.where(lane < 32, value, pltpu.roll(pltpu.roll(value, 32, 1), 4, 0))
        both = jnp.where(lane < 64, pair, pltpu.roll(before, 64, 1))
        out[4 * d : 4 * d + 4, :] = both[:4]
        ends[8 + d : 9 + d, :] = value[0:1]
        before = pair

    shift = jnp.where(patch == 0, PER - LEFT + L, PER - RIGHT + L)
    here, below = ends[8 : 8 + B, :], ends[7 : 7 + B, :]
    lanes = iota((B, L), 1)
    for i in range(2):
        rows = out[pl.ds(i, B, stride=4), :]
        rows = jnp.where(
            (lanes >= PER) & (lanes < PER + 8), pltpu.roll(here, shift - 8 * i, 1), rows
        )
        rows = jnp.where(
            (lanes >= PER + 64) & (lanes < PER + 72), pltpu.roll(below, shift + 64 - 8 * i, 1), rows
        )
        out[pl.ds(i, B, stride=4), :] = rows


def finish_kernel(
    coef, source, inv, h_source, h_inv, colour, known, e_first, e_last, got, out, v_first, h_line
):
    spacing, face = coefficient_rows(coef, Y)
    h_face = coefficient_rows(coef, L)[1]
    left_core = lax.axis_index("gy") == 0
    mine = colour[...]

    upper = iota((8, L), 0) < 4
    tiles = []
    for n in range(B // 2):
        near = got[8 * n : 8 * n + 8, :]
        far = pltpu.roll(near, L - 32, 1)
        tiles.append(jnp.where(upper, near, pltpu.roll(far, 4, 0)))
        tiles.append(jnp.where(upper, pltpu.roll(near, 4, 0), far))
    halves = [jnp.concatenate(tiles[c * L // 8 : (c + 1) * L // 8], 0) for c in range(2)]
    turned = jnp.concatenate([jnp.transpose(half) for half in halves], 1)
    low, high = turned[65 : 65 + X], turned[1 : 1 + X]
    nothing = jnp.zeros((1, L), jnp.float32)
    outer = jnp.where(left_core, tiles[-1], tiles[0])

    def beside(b):
        at_b = 0 if b else 64
        moved = pltpu.roll(outer, L - PER - at_b, 1)
        end = jnp.where(iota((1, L), 1) < 8, moved[0:1], pltpu.roll(moved[1:2], 8, 1))
        lo, hi = turned[at_b : at_b + 1], turned[at_b + 1 + X : at_b + 2 + X]
        places = {XHI: hi[:, :L], XHI + 1: hi[:, L:], XLO0: lo[:, :L], XLO1: lo[:, L:], YH: end}
        return jnp.concatenate([places.get(p, nothing) for p in range(8)], 0)

    beside_after_first(h_face, h_source, h_inv, beside(0), beside(1), h_line)
    columns = sided(transposed(h_line[pl.ds(YH, D, stride=8), :]))
    low_first, high_first = jnp.where(mine == 0, low, 0.0), jnp.where(mine == 0, high, 0.0)
    for k in range(D):
        value = known[at(k), :] + e_first[at(k), :] * low_first
        v_first[at(k), :] = value + e_last[at(k), :] * high_first
    value = low
    for k in range(D - 1):
        added = beside_sum(v_first, h_line, columns, k)
        value = (source[at(k), :] + spacing[k] * added + face[k] * value) * inv[at(k), :]
        out[at(k), :] = value
    value = high
    for k in range(D - 1, -1, -1):
        if k < D - 1:
            value = out[at(k), :] + (face[k + 1] * inv[at(k), :]) * value
        out[at(k), :] = jnp.where(mine == 0, v_first[at(k), :], value)


VMEM = pl.BlockSpec(memory_space=pltpu.VMEM)
ANY = pl.BlockSpec(memory_space=pl.ANY)
SMEM = pl.BlockSpec(memory_space=pltpu.SMEM)


def f32(*shape):
    return jax.ShapeDtypeStruct(shape, jnp.float32)


def call(kernel, outs, specs, scratch, cost, *args, vmem=32):
    return pl.pallas_call(
        kernel,
        out_shape=outs,
        in_specs=specs,
        out_specs=jax.tree.map(lambda _: VMEM, outs),
        scratch_shapes=[
            pltpu.VMEM(s, jnp.float32) if isinstance(s, tuple) else s for s in scratch
        ],
        compiler_params=pltpu.CompilerParams(vmem_limit_bytes=vmem * 1024 * 1024),
        cost_estimate=pl.CostEstimate(flops=cost, bytes_accessed=cost, transcendentals=0),
    )(*args)


def on_device(correction, residual, state, level, colour):
    corr, res, st = (v.reshape(D * X, Y) for v in (correction, residual, state))
    own_lo, own_hi = call(
        pack_x_kernel, (f32(72, Y), f32(72, Y)), [ANY] * 4,
        [pltpu.VMEM((X, Y), jnp.int32), pltpu.SemaphoreType.DMA((9,))],
        1 << 20, correction, residual, state, colour, vmem=60,
    )
    xs = lax.axis_size("gx")
    ring = [(i, (i + 1) % xs) for i in range(xs)]
    got_lo = lax.ppermute(own_hi, "gx", ring)
    got_hi = lax.ppermute(own_lo, "gx", [(b, a) for a, b in ring])
    own_y, tints = call(
        pack_y_kernel, (f32(8, Y), f32(Y, L)), [VMEM] * 4, [], 1 << 20, corr, res, st, colour
    )
    swap = [(0, 1), (1, 0)]
    got_y = lax.ppermute(own_y, "gy", swap)
    field = f32(D * X, Y)
    inv, e_first, e_last, k_own, w_x, w_y, coef = call(
        factor_kernel,
        (field, field, field, f32(3 * X, Y), f32(4 * X, Y), f32(4 * X, Y), f32(40, Y)),
        [SMEM, VMEM], [], 1 << 22, level, st,
    )
    got_lo, got_hi, got_y, inv = lax.optimization_barrier((got_lo, got_hi, got_y, inv))
    crossed = lax.ppermute(jnp.concatenate([got_lo[:D], got_hi[:D]], 0), "gy", swap)
    small = f32(8 * D, L)
    source, v_first, h_local, h_inv, h_first, h_last, h_mask, coupled, laid = call(
        local_kernel, (field, field, small, small, small, small, f32(8, L), f32(Y, L), f32(L, Y)),
        [VMEM] * 16, [(8 * D, L), (8 * D, L), (L, Y)], 1 << 22,
        coef, corr, res, colour, inv, e_first, e_last, k_own, w_x, w_y,
        own_lo, own_hi, got_lo, got_hi, own_y, got_y,
    )
    message, h_source = call(
        message_kernel, (f32(B * R, L), small), [VMEM] * 14, [(8 * D, L), (L, Y)], 1 << 22,
        coef, colour, source, v_first, h_local, h_inv, h_first, h_last, h_mask, coupled, laid,
        e_first, e_last, crossed,
    )

    def exchanged(value, rows):
        blocks = value.reshape(B, rows, L)
        return lax.all_to_all(blocks, "gz", 0, 0, tiled=True).reshape(B * rows, L)

    separators = call(
        separator_kernel, f32(B * 4, L), [VMEM] * 2, [(B + 8, L)],
        1 << 21, exchanged(message, R), tints,
    )
    out = call(
        finish_kernel, field, [VMEM] * 10, [(D * X, Y), (8 * D, L)], 1 << 21,
        coef, source, inv, h_source, h_inv, colour, v_first, e_first, e_last,
        exchanged(separators, 4),
    )
    return out.reshape(D, X, Y)


def solution(mesh):
    block = P("gz", "gx", "gy")
    return jax.shard_map(
        on_device,
        mesh=mesh,
        in_specs=(block, block, block, P(), P("gx", "gy")),
        out_specs=block,
        check_vma=False,
    )
```
